512 devices in a mesh: sub: 32 (over y, x), clu: 16 (over z, core).
Axes of the slice: x: 4, y: 8, z: 8, core: 2. Of those that a mesh axis runs over, the one named last changes fastest.
Arguments:
- dual_ops: bfloat16 [16, 32, 1536, 1536], P('clu', 'sub'), may hold values from -60 to 60, as said below
- neighbors: int32 [16, 32, 4], P('clu', 'sub'), may hold values from 0 to 31, as said below
- face_counts: int32 [16, 32, 6], P('clu', 'sub'), may hold values from 0 to 256, as said below
- load_terms: float32 [16, 32, 6, 256], P('clu', 'sub'), may hold values from -10 to 10
- precond_terms: float32 [16, 32, 6, 256], P('clu', 'sub'), may hold values from 0.25 to 2
- rigid_terms: float32 [16, 32, 6, 6, 256], P('clu', 'sub'), may hold values from -6 to 6
- recycled_terms: bfloat16 [16, 32, 64, 6, 256], P('clu', 'sub'), may hold values from -6 to 6
Outputs:
- dual_solution: float32 [16, 32, 6, 256], P('clu', 'sub')
- residual: float32 [16, 32, 6, 256], P('clu', 'sub')
The draws below stay inside these ranges and needn't reach their ends.
Inputs may be any that keep to these rules, and one draw needn't show every extreme that they name: `neighbors`: faces 0 to 3 of subdomain i name four different other subdomains of its cluster, and each such subdomain names i on one of its faces 0 to 3. `face_counts`: both copies of an interface have the same count; faces 4 of the first cluster and faces 5 of the last have none; some face has 256. Each dual_ops[c, i] is positive definite.
All inputs are finite; a program needn't handle non-finite values.
Results may differ from the reference program's by a relative error of at most 0.014.
Values sent between devices are 32-bit elements; how exact they have to be, the bound alone decides.
No kernel may reach another device: no remote copies, remote signals or barrier semaphores. Data moves between devices by JAX's collectives and lax.ppermute only.
A program may use at most 64 MiB of HBM per device.

```python
import math
import jax
import jax.numpy as jnp
from jax import lax

FACE = 256
RECYC = 64
ITERS = 3
NSD = 32
NCL = 16


def interface_layout(key):
    label_keys = jax.random.split(jax.random.fold_in(key, 101), NCL)
    mask_keys = jax.random.split(jax.random.fold_in(key, 102), NCL)
    labels = jax.vmap(lambda subkey: jax.random.permutation(subkey, NSD))(label_keys).astype(jnp.int32)
    xor_masks = jax.vmap(lambda subkey: jax.random.permutation(subkey, NSD - 1)[:4] + 1)(mask_keys).astype(jnp.int32)
    face_loads = jax.random.randint(jax.random.fold_in(key, 103), (NCL, 4, NSD), FACE // 2, FACE + 1)
    face_loads = face_loads.at[:, :, 0].set(FACE)
    across = jax.random.randint(jax.random.fold_in(key, 104), (NCL + 1, NSD), FACE // 2, FACE + 1)
    across = across.at[0].set(0).at[NCL].set(0)
    places = jnp.argsort(labels, axis=1).astype(jnp.int32)
    partners = jnp.bitwise_xor(places[:, :, None], xor_masks[:, None, :])
    neighbor_ids = jax.vmap(lambda label_row, other_row: label_row[other_row])(labels, partners)
    lowest = jnp.minimum(places[:, :, None], partners)
    face_rows = jnp.arange(4, dtype=jnp.int32)[None, :]
    inner_counts = jax.vmap(lambda load_table, lowest_row: load_table[face_rows, lowest_row])(face_loads, lowest)
    counts = jnp.concatenate([inner_counts, across[:-1, :, None], across[1:, :, None]], axis=2)
    return (neighbor_ids.astype(jnp.int32), counts.astype(jnp.int32))


def rigid_layout(key, rim_scale):
    base_values = jax.random.normal(jax.random.fold_in(key, 201), (NCL, NSD, 6, 6, FACE), jnp.float32)
    face_scale = jnp.where(jnp.arange(6) < 4, 1.0, rim_scale).astype(jnp.float32)
    rigid_values = base_values * face_scale[None, None, None, :, None]
    rigid_values = rigid_values.at[1:, :, :, 4].set(rigid_values[:-1, :, :, 5])
    return jnp.clip(rigid_values, -6.0, 6.0)


def draw_neighbors(key, part):
    return interface_layout(key)[0]


def draw_face_counts(key, part):
    return interface_layout(key)[1]


def draw_rigid_terms(key, part):
    rim_scale = 1.5
    return rigid_layout(key, rim_scale)


def draw_load_terms(key, part):
    rim_scale = 1.5
    rigid_values = rigid_layout(key, rim_scale)
    key = jax.random.fold_in(key, 41)
    signs = 2.0 * jax.random.randint(jax.random.fold_in(key, 1), (NCL, 1, 6), 0, 2).astype(jnp.float32) - 1.0
    magnitudes = jnp.exp(jax.random.uniform(jax.random.fold_in(key, 2), (NCL, NSD, 6), jnp.float32, math.log(0.5), math.log(2.0)))
    coefs = signs * magnitudes
    noise_part = jax.random.normal(jax.random.fold_in(key, 3), (NCL, NSD, 6, FACE), jnp.float32)
    combined = noise_part
    for mode_index in range(6):
        combined = combined + coefs[:, :, mode_index, None, None] * rigid_values[:, :, mode_index]
    return jnp.clip(combined, -10.0, 10.0)


def draw_recycled_terms(key, part):
    rim_scale = 1.5
    rigid_values = rigid_layout(key, rim_scale)
    key = jax.random.fold_in(key, 31)
    mix_weights = 0.5 * jax.random.normal(jax.random.fold_in(key, 1), (NCL, RECYC, 6), jnp.float32)
    noise_part = 0.5 * jax.random.normal(jax.random.fold_in(key, 2), (NCL, NSD, RECYC, 6, FACE), jnp.float32)
    combined = noise_part
    for mode_index in range(6):
        combined = combined + mix_weights[:, None, :, mode_index, None, None] * rigid_values[:, :, mode_index][:, :, None]
    return jnp.clip(combined, -6.0, 6.0).astype(jnp.bfloat16)


def draw_dual_ops(key, part):
    key = jax.random.fold_in(key, 11)
    order_full = 6 * FACE
    low_end, high_end = (0.5, 2.0)
    spread = 0.36 / math.sqrt(order_full)

    def one_matrix(subkey):
        key_off, key_diag, key_scale, key_stiff = jax.random.split(subkey, 4)
        uniform_part = jax.random.uniform(key_off, (order_full, order_full), jnp.float32, -1.0, 1.0)
        off_diagonal = (uniform_part + uniform_part.T) * spread
        diagonal = jax.random.uniform(key_diag, (order_full,), jnp.float32, 1.0, 2.0)
        scales = jnp.exp(jax.random.uniform(key_scale, (order_full,), jnp.float32, math.log(low_end), math.log(high_end)))
        stiffness = jnp.exp(jax.random.uniform(key_stiff, (), jnp.float32, math.log(0.3), math.log(3.0)))
        eye_mask = jnp.eye(order_full, dtype=jnp.float32)
        matrix = off_diagonal * (1.0 - eye_mask) + eye_mask * diagonal[None, :]
        return (stiffness * scales[:, None] * matrix * scales[None, :]).astype(jnp.bfloat16)
    subkeys = jax.random.split(key, NCL * NSD)
    return lax.map(one_matrix, subkeys).reshape(NCL, NSD, order_full, order_full)


def steps_of(own_key, extent, shards, smallest, top_value):
    factor_of, own = 1.0, jax.random.fold_in(own_key, 6)
    for dim, parts in shards:
        heights = jnp.exp(jax.random.uniform(jax.random.fold_in(own, dim), (parts,), jnp.float32, smallest / len(shards), top_value / len(shards)))
        factor_of = factor_of * jnp.repeat(heights, extent[dim] // parts).reshape([-1 if axis == dim else 1 for axis in range(len(extent))])
    return factor_of


def setup_inputs(seed: int = 0) -> dict:
    key_of = jax.random.split(jax.random.key(seed), 8)
    dual_ops = draw_dual_ops(jax.random.fold_in(key_of[7], 71), 0)
    neighbors = draw_neighbors(jax.random.fold_in(key_of[7], 71), 0)
    face_counts = draw_face_counts(jax.random.fold_in(key_of[7], 71), 0)
    load_terms = draw_load_terms(jax.random.fold_in(key_of[7], 71), 0)
    precond_terms = jnp.clip(jnp.exp(math.log(2.0) - 2.0794415 * jax.random.uniform(key_of[4], (NCL, NSD, 6, FACE), jnp.float32) ** steps_of(key_of[4], (NCL, NSD, 6, FACE), ((0, 16), (1, 32)), -0.2, 0.2)), 0.25, 2.0)
    rigid_terms = draw_rigid_terms(jax.random.fold_in(key_of[7], 71), 0)
    recycled_terms = draw_recycled_terms(jax.random.fold_in(key_of[7], 71), 0)
    return {"dual_ops": dual_ops, "neighbors": neighbors, "face_counts": face_counts, "load_terms": load_terms, "precond_terms": precond_terms, "rigid_terms": rigid_terms, "recycled_terms": recycled_terms}


precise = lax.Precision.HIGHEST

def partner_copy(values, neighbors):
    cluster_ids = jnp.arange(NCL, dtype=jnp.int32)[:, None]
    own_ids = jnp.arange(NSD, dtype=jnp.int32)
    face_list = []
    for face_index in range(4):
        peer_ids = neighbors[:, :, face_index]
        gathered = values[cluster_ids, peer_ids]
        back_list = neighbors[cluster_ids, peer_ids]
        select = (back_list == own_ids[None, :, None]).astype(jnp.float32)
        face_list.append(jnp.einsum('cnk,cnlkf->cnlf', select, gathered[:, :, :, :4, :], precision=precise))
    blank_rows = jnp.zeros_like(values[:1, :, :, 0, :])
    face_list.append(jnp.concatenate([blank_rows, values[:-1, :, :, 5, :]], axis=0))
    face_list.append(jnp.concatenate([values[1:, :, :, 4, :], blank_rows], axis=0))
    return jnp.stack(face_list, axis=3)

def coarse_sum(rigid_cols, values, factor):
    partial_value = jnp.einsum('cnjrfs,cnlfs->cjrl', rigid_cols, values, precision=precise)
    padded = jnp.zeros((NCL + 2, 6, values.shape[2]), jnp.float32)
    for offset in range(3):
        padded = padded.at[offset:offset + NCL].add(partial_value[:, offset])
    return factor * padded[1:NCL + 1].reshape(NCL * 6, values.shape[2])

def coarse_apply(rigid_cols, amounts):
    columns = amounts.shape[1]
    blocks = amounts.reshape(NCL, 6, columns)
    blank_rows = jnp.zeros((1, 6, columns), jnp.float32)
    padded = jnp.concatenate([blank_rows, blocks, blank_rows], axis=0)
    nearby = jnp.stack([padded[offset:offset + NCL] for offset in range(3)], axis=1)
    return jnp.einsum('cnjrfs,cjrl->cnlfs', rigid_cols, nearby, precision=precise)

def gram_matrix(rigid_cols):
    partial_value = jnp.einsum('cnjrfs,cnkqfs->cjrkq', rigid_cols, rigid_cols, precision=precise).reshape(NCL, 18, 18)
    full_matrix = jnp.zeros((6 * NCL + 12, 6 * NCL + 12), jnp.float32)
    for cluster in range(NCL):
        full_matrix = full_matrix.at[6 * cluster:6 * cluster + 18, 6 * cluster:6 * cluster + 18].add(partial_value[cluster])
    return 0.5 * full_matrix[6:6 + 6 * NCL, 6:6 + 6 * NCL]

def spd_solve(matrix, right_side):
    factor_low = jnp.linalg.cholesky(matrix)
    halfway = lax.linalg.triangular_solve(factor_low, right_side, left_side=True, lower=True)
    return lax.linalg.triangular_solve(factor_low, halfway, left_side=True, lower=True, transpose_a=True)

def half_dot(first, second):
    return 0.5 * jnp.einsum('cnafs,cnbfs->ab', first, second, precision=precise)

def apply_ops(values, dual_ops):
    columns = values.shape[2]
    flat_rows = values.reshape(NCL * NSD, columns, 6 * FACE)
    op_rows = dual_ops.reshape(NCL * NSD, 6 * FACE, 6 * FACE)
    result = lax.map(lambda operands: jnp.dot(operands[0].astype(jnp.float32), operands[1].astype(jnp.float32), preferred_element_type=jnp.float32), (flat_rows, op_rows))
    return result.reshape(NCL, NSD, columns, 6, FACE)

def reference(dual_ops, neighbors, face_counts, load_terms, precond_terms, rigid_terms, recycled_terms):
    live_slots = (jnp.arange(FACE, dtype=jnp.int32)[None, None, None, :] < face_counts[:, :, :, None]).astype(jnp.float32)[:, :, None]
    face_index = jnp.arange(6, dtype=jnp.int32)
    inner_face = (face_index < 4).astype(jnp.float32)[:, None]
    below_face = (face_index == 4).astype(jnp.float32)[:, None]
    above_face = (face_index == 5).astype(jnp.float32)[:, None]
    stacked = jnp.concatenate([load_terms[:, :, None], precond_terms[:, :, None], rigid_terms, recycled_terms.astype(jnp.float32)], axis=2)
    copies = partner_copy(stacked, neighbors)
    demand = live_slots * (load_terms[:, :, None] + copies[:, :, 0:1])
    weights = 0.5 * live_slots * (precond_terms[:, :, None] + copies[:, :, 1:2])
    rigid_copy = copies[:, :, 2:8]
    rigid_cols = jnp.stack([live_slots * rigid_copy * below_face, live_slots * (rigid_terms + rigid_copy * inner_face), live_slots * rigid_copy * above_face], axis=2)
    basis_raw = live_slots * (recycled_terms.astype(jnp.float32) + copies[:, :, 8:])
    coarse_matrix = gram_matrix(rigid_cols)

    def project(values):
        return values - coarse_apply(rigid_cols, spd_solve(coarse_matrix, coarse_sum(rigid_cols, values, 0.5)))

    def assemble(values):
        return live_slots * (values + partner_copy(values, neighbors))
    basis_vec = project(basis_raw)
    start_res = project(demand)
    images = assemble(live_slots * apply_ops(basis_vec.astype(jnp.bfloat16), dual_ops))
    deflated = project(images)
    energy = half_dot(basis_vec, images)
    energy = 0.5 * (energy + energy.T)
    amount = spd_solve(energy, half_dot(basis_vec, start_res))
    solution = jnp.einsum('cnlfs,lk->cnkfs', basis_vec, amount, precision=precise)
    residual = start_res - jnp.einsum('cnlfs,lk->cnkfs', deflated, amount, precision=precise)

    def precondition(current):
        search = project(weights * current)
        rho_value = half_dot(current, search)[0, 0]
        deflate_coeff = spd_solve(energy, half_dot(deflated, search))
        return (search, rho_value, deflate_coeff)
    search, rho_now, deflate_coeff = precondition(residual)
    direction = search - jnp.einsum('cnlfs,lk->cnkfs', basis_vec, deflate_coeff, precision=precise)
    for iteration in range(ITERS):
        image_vec = project(assemble(live_slots * apply_ops(direction.astype(jnp.bfloat16), dual_ops)))
        step_size = rho_now / half_dot(direction, image_vec)[0, 0]
        solution = solution + step_size * direction
        residual = residual - step_size * image_vec
        if iteration + 1 < ITERS:
            search, rho_next, deflate_coeff = precondition(residual)
            direction = search - jnp.einsum('cnlfs,lk->cnkfs', basis_vec, deflate_coeff, precision=precise) + rho_next / rho_now * direction
            rho_now = rho_next
    return (solution[:, :, 0], residual[:, :, 0])
```

```python
import jax
import jax.numpy as jnp
from jax import lax
from jax.experimental import pallas as pl
from jax.experimental.pallas import tpu as pltpu
from jax.sharding import PartitionSpec as P

ITERS = 3
LANES = 128


precise = lax.Precision.HIGHEST


def dot(first, second):
    return jnp.dot(first, second, precision=precise, preferred_element_type=jnp.float32)


def dot_t(first, second):
    return lax.dot_general(
        first, second, (((1,), (1,)), ((), ())), precision=precise, preferred_element_type=jnp.float32
    )


def padded_row(values, multiple=LANES):
    flat = values.reshape(-1)
    return jnp.pad(flat, (0, -flat.shape[0] % multiple))


def everyone(row, axis):
    count = lax.axis_size(axis)
    sent = jnp.broadcast_to(row[None, None, :], (count, 1, row.shape[0]))
    return lax.all_to_all(sent, axis, split_axis=0, concat_axis=0, tiled=True)[:, 0, :]


def trade(rows, axis):
    return lax.all_to_all(rows[:, None, :], axis, split_axis=0, concat_axis=0, tiled=True)[:, 0, :]


def rims(values):
    count = lax.axis_size("clu")
    forward = [(i, i + 1) for i in range(count - 1)]
    backward = [(i + 1, i) for i in range(count - 1)]
    low = lax.ppermute(values[:, 5, :], "clu", forward)
    high = lax.ppermute(values[:, 4, :], "clu", backward)
    return low, high


def six_faces(inner, low, high):
    return jnp.concatenate([inner, low[:, None, :], high[:, None, :]], axis=1)


def invert(matrix_ref, inverse_ref):
    size = matrix_ref.shape[0]
    rows = lax.broadcasted_iota(jnp.int32, (size, size), 0)
    lanes = lax.broadcasted_iota(jnp.int32, (size, size), 1)
    row_lanes = lax.broadcasted_iota(jnp.int32, (1, size), 1)
    column_rows = lax.broadcasted_iota(jnp.int32, (size, 1), 0)
    values = matrix_ref[...]
    for k in range(size):
        pivot_row = values[k : k + 1, :]
        reciprocal = 1.0 / pivot_row[:, k : k + 1]
        scaled_row = jnp.where(row_lanes == k, 1.0, pivot_row) * reciprocal
        column = jnp.where(column_rows == k, -1.0, values[:, k : k + 1])
        kept = jnp.where((rows == k) | (lanes == k), 0.0, values)
        values = kept - column * scaled_row
    inverse_ref[...] = values


def spd_inverse(matrix):
    size = matrix.shape[0]
    return pl.pallas_call(
        invert,
        out_shape=jax.ShapeDtypeStruct((size, size), jnp.float32),
        in_specs=[pl.BlockSpec(memory_space=pltpu.VMEM)],
        out_specs=pl.BlockSpec(memory_space=pltpu.VMEM),
        cost_estimate=pl.CostEstimate(flops=2 * size**3, bytes_accessed=8 * size**2, transcendentals=size),
    )(matrix)


def local(dual_ops, neighbors, face_counts, load_terms, precond_terms, rigid_terms, recycled_terms):
    local_op = dual_ops[0, 0]
    neighbor_ids = neighbors[0, 0]
    load = load_terms[0, 0]
    rigid = rigid_terms[0, 0]
    recycled = recycled_terms[0, 0].astype(jnp.float32)
    clusters = lax.axis_size("clu")
    members = lax.axis_size("sub")
    clu_index = lax.axis_index("clu")
    sub_index = lax.axis_index("sub")
    slots = load.shape[-1]
    width = 6 * slots
    count = recycled.shape[0]
    per = count // members
    piece = 4 * per * slots
    coarse = 6 * clusters
    onehot = (neighbor_ids[:, None] == jnp.arange(members, dtype=jnp.int32)[None, :]).astype(
        jnp.float32
    )
    live = (
        jnp.arange(slots, dtype=jnp.int32)[None, :] < face_counts[0, 0][:, None]
    ).astype(jnp.float32)
    flat_live = live.reshape(1, width)

    targets = jnp.arange(coarse, dtype=jnp.int32)[:, None]
    sources = jnp.arange(18 * clusters, dtype=jnp.int32)[None, :]
    spread = (
        targets == 6 * (sources // 18) + (sources % 18) - 6
    ).astype(jnp.float32)
    spread_back = spread.T.reshape(clusters, 18, coarse)

    def nearby(values):
        padded = jnp.pad(values, ((6, 6), (0, 0)))
        return lax.dynamic_slice_in_dim(padded, 6 * clu_index, 18, 0)

    def to_carriers(values):
        faces = values.reshape(members, per, 6, slots)[:, :, :4]
        return faces.transpose(0, 2, 1, 3).reshape(members, piece)

    def from_carriers(received):
        faces = received.reshape(members, 4, per, slots).transpose(0, 2, 1, 3)
        return faces.reshape(count, 4, slots)

    few = jnp.concatenate([load[None], precond_terms[0, 0][None], rigid], axis=0)
    few_count = few.shape[0]
    low, high = rims(jnp.concatenate([few, recycled], axis=0))
    direct = dot(onehot.T, few[:, :4].transpose(1, 0, 2).reshape(4, few_count * slots))
    ids = jnp.broadcast_to(padded_row(neighbor_ids.astype(jnp.float32))[None], (members, LANES))
    received = trade(jnp.concatenate([to_carriers(recycled), direct, ids], axis=1), "sub")
    table = received[:, piece + few_count * slots :][:, :4]
    slots_of = 4 * members
    row_member = (lax.broadcasted_iota(jnp.int32, (slots_of, slots_of), 0) // 4).astype(jnp.float32)
    lane_member = (lax.broadcasted_iota(jnp.int32, (slots_of, slots_of), 1) // 4).astype(jnp.float32)
    route = jnp.where(
        (table.reshape(slots_of, 1) == lane_member) & (table.reshape(1, slots_of) == row_member), 1.0, 0.0
    )

    def carry(arrived):
        return dot(route, arrived.reshape(4 * members, per * slots)).reshape(members, piece)

    few_inner = dot(onehot, received[:, piece : piece + few_count * slots])
    few_inner = few_inner.reshape(4, few_count, slots).transpose(1, 0, 2)
    few_copy = six_faces(few_inner, low[:few_count], high[:few_count])
    demand = (live * (load + few_copy[0])).reshape(1, width)
    weights = (0.5 * live * (few[1] + few_copy[1])).reshape(1, width)
    face_index = jnp.arange(6, dtype=jnp.int32)
    inner_face = (face_index < 4).astype(jnp.float32)[:, None]
    below_face = (face_index == 4).astype(jnp.float32)[:, None]
    above_face = (face_index == 5).astype(jnp.float32)[:, None]
    rigid_copy = few_copy[2:]
    cols = jnp.concatenate(
        [
            live * rigid_copy * below_face,
            live * (rigid + rigid_copy * inner_face),
            live * rigid_copy * above_face,
        ],
        axis=0,
    ).reshape(18, width)
    weighted_cols = weights * cols
    flat_recycled = recycled.reshape(count, width)
    sums = dot_t(
        cols,
        jnp.concatenate(
            [0.5 * cols, 0.5 * weighted_cols, flat_recycled, load.reshape(1, width)], axis=0
        ),
    )
    sums_size = sums.size
    sums_row = padded_row(sums)
    received = trade(
        jnp.concatenate(
            [carry(received[:, :piece]), jnp.broadcast_to(sums_row[None], (members, sums_row.shape[0]))],
            axis=1,
        ),
        "sub",
    )
    basis_raw = (
        live * (recycled + six_faces(from_carriers(received[:, :piece]), low[few_count:], high[few_count:]))
    ).reshape(count, width)
    gathered = everyone(jnp.sum(received[:, piece:], axis=0), "clu")
    gathered = gathered[:, :sums_size].reshape(clusters, 18, 37 + count)
    pairs = jnp.einsum(
        "cgab,cbx->cagx",
        jnp.stack([gathered[:, :, :18], gathered[:, :, 18:36]], axis=1),
        spread_back,
        precision=precise,
    ).reshape(18 * clusters, 2 * coarse)
    assembled = dot(
        spread,
        jnp.concatenate([pairs, gathered[:, :, 36:].reshape(18 * clusters, count + 1)], axis=1),
    )
    coarse_inverse = spd_inverse(assembled[:, :coarse])
    weighted_matrix = assembled[:, coarse : 2 * coarse]
    amounts = nearby(dot(coarse_inverse, assembled[:, 2 * coarse :]))
    projected = jnp.concatenate([basis_raw, demand], axis=0) - dot(amounts.T, cols)
    basis = projected[:count]
    start = projected[count:]

    products = flat_live * jnp.dot(
        basis.astype(jnp.bfloat16), local_op, preferred_element_type=jnp.float32
    )
    low, high = rims(products.reshape(count, 6, slots))
    both_cols = jnp.concatenate([cols, weighted_cols], axis=0)
    grouped = both_cols.reshape(2, 3, 6, width).transpose(0, 2, 1, 3).reshape(12, 3, width)
    grouped = jnp.pad(grouped, ((0, 0), (0, 1), (0, 0))).reshape(48, width)
    tests = jnp.concatenate([basis, grouped], axis=0)
    sums = dot_t(tests, products)
    start_row = dot_t(0.5 * start, tests)
    basis_parts = count // 4
    shares = jnp.concatenate(
        [
            sums.reshape(basis_parts + 12, 4 * count),
            jnp.pad(start_row[:, :count], ((0, 0), (0, 3 * count))),
            jnp.pad(start_row[:, count:], ((0, 0), (0, 4 * count - 48))),
            jnp.zeros((members - basis_parts - 14, 4 * count), jnp.float32),
        ],
        axis=0,
    )
    received = trade(
        jnp.concatenate([to_carriers(products), shares], axis=1), "sub"
    )
    share = everyone(jnp.sum(received[:, piece:], axis=0), "clu").reshape(clusters, 4, count)
    whole = jnp.pad(jnp.sum(share, axis=0), ((0, clusters - 4), (0, 0)))
    beside = jnp.pad(share[:, :3], ((1, 1), (0, 0), (0, 0)))
    shifted = beside[2:, 0] + beside[1:-1, 1] + beside[:-2, 2]
    is_coarse = (sub_index >= basis_parts) & (sub_index < basis_parts + 12)
    is_listed = sub_index == basis_parts + 13
    share = jnp.where(is_coarse, shifted, jnp.where(is_listed, share[:, 0], whole))
    share_size = clusters * count
    received = trade(
        jnp.concatenate(
            [
                carry(received[:, :piece]),
                jnp.broadcast_to(share.reshape(1, share_size), (members, share_size)),
            ],
            axis=1,
        ),
        "sub",
    )
    images = (
        live
        * (products.reshape(count, 6, slots) + six_faces(from_carriers(received[:, :piece]), low, high))
    ).reshape(count, width)
    parts = received[:, piece:].reshape(members, clusters, count)
    energy_raw = parts[:basis_parts, :4].reshape(count, count)
    image_coarse = parts[basis_parts : basis_parts + 6].transpose(1, 0, 2).reshape(coarse, count)
    image_weighted = parts[basis_parts + 6 : basis_parts + 12].transpose(1, 0, 2).reshape(coarse, count)
    start_sums = parts[basis_parts + 12, 0][:, None]
    listed = parts[basis_parts + 13, :, 24:48].reshape(clusters, 6, 4)[:, :, :3]
    start_weighted = dot(spread, listed.transpose(0, 2, 1).reshape(18 * clusters, 1))
    energy_inverse = spd_inverse(0.5 * (energy_raw + energy_raw.T))
    amount = dot(energy_inverse, start_sums)

    mixed = dot(amount.T, jnp.concatenate([basis, images], axis=1))
    solution = mixed[:, :width]
    shift = dot(coarse_inverse, dot(image_coarse, amount))
    residual = start - mixed[:, width:] + dot(nearby(shift).T, cols)
    weighted_residual = start_weighted - dot(image_weighted, amount) + dot(weighted_matrix, shift)
    amounts = dot(coarse_inverse, weighted_residual)
    search = weights * residual - dot(nearby(amounts).T, cols)
    weighted_images = weights * images
    parts_mixed = jnp.concatenate([cols, basis], axis=0)
    weighted_inverse = dot(coarse_inverse, weighted_matrix)
    by_shift = dot(energy_inverse, image_weighted.T)
    by_amounts = dot(energy_inverse, image_coarse.T)

    sums_row = padded_row(
        dot_t(jnp.concatenate([products, 0.5 * residual], axis=0), weights * residual)
    )
    received = everyone(
        jnp.concatenate([sums_row, weights[0, : 4 * slots]]), "sub"
    )
    all_weights = received[:, LANES:].reshape(slots_of, slots)
    totals = jnp.sum(
        everyone(jnp.sum(received[:, :LANES], axis=0), "clu"), axis=0, keepdims=True
    )
    rho = totals[:, count : count + 1]
    coeff = dot(energy_inverse, totals[:, :count].T) - dot(by_amounts, amounts)
    deflated_search = search - dot(coeff.T, basis)
    direction = deflated_search
    for iteration in range(ITERS):
        last = iteration + 1 == ITERS
        product = flat_live * jnp.dot(
            direction.astype(jnp.bfloat16), local_op, preferred_element_type=jnp.float32
        )
        faces = product.reshape(6, slots)
        low, high = rims(faces[None])
        tests = [both_cols, direction]
        if not last:
            tests += [weights * residual, weighted_images]
        sums = dot_t(product, jnp.concatenate(tests, axis=0))
        if not last:
            beside = jnp.concatenate([jnp.zeros((1, 4 * slots), jnp.float32), low, high], axis=1)
            square = jnp.sum(weights * product * (product + beside), axis=1, keepdims=True)
            sums = jnp.concatenate([sums, square], axis=1)
        received = everyone(
            jnp.concatenate([product[0, : 4 * slots], padded_row(sums)]), "sub"
        )
        all_faces = received[:, : 4 * slots].reshape(slots_of, slots)
        all_partners = dot(route, all_faces)
        inner = lax.dynamic_slice_in_dim(all_partners, 4 * sub_index, 4, 0)
        assembled = (live * (faces + jnp.concatenate([inner, low, high], axis=0))).reshape(1, width)
        sums = jnp.sum(received[:, 4 * slots :], axis=0, keepdims=True)
        if not last:
            cross = jnp.sum(
                jnp.sum(all_weights * all_faces * all_partners, axis=0, keepdims=True),
                axis=1,
                keepdims=True,
            )
            lane = lax.broadcasted_iota(jnp.int32, sums.shape, 1)
            sums = sums + jnp.where(lane == 38 + count, cross, 0.0)
        gathered = everyone(sums[0], "clu")
        pair = dot(
            spread,
            gathered[:, :36].reshape(clusters, 2, 18).transpose(0, 2, 1).reshape(18 * clusters, 2),
        )
        totals = jnp.sum(gathered, axis=0, keepdims=True)
        step = rho / totals[:, 36:37]
        shifts = dot(coarse_inverse, pair)
        shift = shifts[:, :1]
        if last:
            image = assembled - dot(nearby(shift).T, cols)
            solution = solution + step * direction
            residual = residual - step * image
            break
        turned = shifts[:, 1:] - dot(weighted_inverse, shift)
        coeff_change = (
            dot(energy_inverse, totals[:, 38 : 38 + count].T)
            - dot(by_shift, shift)
            - dot(by_amounts, turned)
        )
        near = nearby(jnp.concatenate([shift, turned], axis=1))
        mixed = dot(
            jnp.concatenate([near, jnp.concatenate([jnp.zeros_like(coeff_change), coeff_change], axis=1)], axis=0).T,
            parts_mixed,
        )
        image = assembled - mixed[:1]
        cross = totals[:, 37:38] - dot(shift.T, weighted_residual)
        weighted_shift = dot(weighted_matrix, shift)
        square = totals[:, 38 + count : 39 + count] - dot(shift.T, 2.0 * pair[:, 1:] - weighted_shift)
        rho_next = rho - step * (2.0 * cross - step * square)
        weighted_residual = weighted_residual - step * (pair[:, 1:] - weighted_shift)
        solution = solution + step * direction
        residual = residual - step * image
        deflated_search = deflated_search - step * (weights * image - mixed[1:])
        direction = deflated_search + rho_next / rho * direction
        rho = rho_next
    return (solution.reshape(1, 1, 6, slots), residual.reshape(1, 1, 6, slots))


def solution(mesh):
    return jax.shard_map(
        local,
        mesh=mesh,
        in_specs=(
            P("clu", "sub", None, None),
            P("clu", "sub", None),
            P("clu", "sub", None),
            P("clu", "sub", None, None),
            P("clu", "sub", None, None),
            P("clu", "sub", None, None, None),
            P("clu", "sub", None, None, None),
        ),
        out_specs=(P("clu", "sub", None, None), P("clu", "sub", None, None)),
        check_vma=False,
    )
```

```python
import functools

import jax
import jax.numpy as jnp
from jax import lax
from jax.experimental import pallas as pl
from jax.experimental.pallas import tpu as pltpu
from jax.sharding import PartitionSpec as P

ITERS = 3
LANES = 128


precise = lax.Precision.HIGHEST


def dot(first, second):
    return jnp.dot(first, second, precision=precise, preferred_element_type=jnp.float32)


def dot_t(first, second):
    return lax.dot_general(
        first, second, (((1,), (1,)), ((), ())), precision=precise, preferred_element_type=jnp.float32
    )


def padded_row(values, multiple=LANES):
    flat = values.reshape(-1)
    return jnp.pad(flat, (0, -flat.shape[0] % multiple))


def everyone(row, axis):
    count = lax.axis_size(axis)
    sent = jnp.broadcast_to(row[None, None, :], (count, 1, row.shape[0]))
    return lax.all_to_all(sent, axis, split_axis=0, concat_axis=0, tiled=True)[:, 0, :]


def trade(rows, axis):
    return lax.all_to_all(rows[:, None, :], axis, split_axis=0, concat_axis=0, tiled=True)[:, 0, :]


def rims(values):
    count = lax.axis_size("clu")
    forward = [(i, i + 1) for i in range(count - 1)]
    backward = [(i + 1, i) for i in range(count - 1)]
    low = lax.ppermute(values[:, 5, :], "clu", forward)
    high = lax.ppermute(values[:, 4, :], "clu", backward)
    return low, high


def six_faces(inner, low, high):
    return jnp.concatenate([inner, low[:, None, :], high[:, None, :]], axis=1)


def invert(matrix_ref, inverse_ref):
    size = matrix_ref.shape[0]
    rows = lax.broadcasted_iota(jnp.int32, (size, size), 0)
    lanes = lax.broadcasted_iota(jnp.int32, (size, size), 1)
    row_lanes = lax.broadcasted_iota(jnp.int32, (1, size), 1)
    column_rows = lax.broadcasted_iota(jnp.int32, (size, 1), 0)
    values = matrix_ref[...]
    for k in range(0, size, 2):
        first, second = values[k : k + 1, :], values[k + 1 : k + 2, :]
        across = second[:, k : k + 1]
        first_part = 1.0 / first[:, k : k + 1]
        ratio = across * first_part
        second_part = 1.0 / (second[:, k + 1 : k + 2] - ratio * across)
        mixed_part = ratio * second_part
        here, after = row_lanes == k, row_lanes == k + 1
        first = jnp.where(here, 1.0, jnp.where(after, 0.0, first))
        second = jnp.where(after, 1.0, jnp.where(here, 0.0, second))
        first_scaled = (first_part + ratio * mixed_part) * first - mixed_part * second
        second_scaled = second_part * second - mixed_part * first
        here, after = column_rows == k, column_rows == k + 1
        first_column = jnp.where(here, -1.0, jnp.where(after, 0.0, values[:, k : k + 1]))
        second_column = jnp.where(after, -1.0, jnp.where(here, 0.0, values[:, k + 1 : k + 2]))
        kept = jnp.where((rows // 2 == k // 2) | (lanes // 2 == k // 2), 0.0, values)
        values = kept - first_column * first_scaled - second_column * second_scaled
    inverse_ref[...] = values


def spd_inverse(matrix):
    size = matrix.shape[0]
    return pl.pallas_call(
        invert,
        out_shape=jax.ShapeDtypeStruct((size, size), jnp.float32),
        in_specs=[pl.BlockSpec(memory_space=pltpu.VMEM)],
        out_specs=pl.BlockSpec(memory_space=pltpu.VMEM),
        cost_estimate=pl.CostEstimate(flops=2 * size**3, bytes_accessed=8 * size**2, transcendentals=size),
    )(matrix)


PARTS = 4
VMEM = pl.BlockSpec(memory_space=pltpu.VMEM)


def lane_sum(values):
    return jnp.sum(values, axis=1, keepdims=True)


def row_sum(values):
    return jnp.sum(values, axis=0, keepdims=True)


def advance(count, gathered, image_sum, state, state_out, weighted, rho, weighted_out, rho_out, refs, again):
    spread, mask, by_coarse, by_weighted, by_products, cols, basis, weights = refs
    coarse = weighted.shape[0]
    near = cols.shape[0]
    values = gathered[:, :LANES]
    high = values.astype(jnp.bfloat16)
    rest = values - high.astype(jnp.float32)
    middle = rest.astype(jnp.bfloat16)
    low = (rest - middle.astype(jnp.float32)).astype(jnp.bfloat16)
    lifted = (
        jnp.dot(high, spread[...], preferred_element_type=jnp.float32)
        + jnp.dot(middle, spread[...], preferred_element_type=jnp.float32)
        + jnp.dot(low, spread[...], preferred_element_type=jnp.float32)
    )
    lifted = row_sum(lifted * mask[...])
    coarse_row = lifted[:, :LANES] + lifted[:, LANES : 2 * LANES] + lifted[:, 2 * LANES : 3 * LANES]
    weighted_row = (
        lifted[:, 3 * LANES : 4 * LANES] + lifted[:, 4 * LANES : 5 * LANES] + lifted[:, 5 * LANES :]
    )
    totals = row_sum(values)
    step = rho[...] / totals[:, 36:37]
    from_coarse = lane_sum(by_coarse[...] * coarse_row)
    from_weighted = lane_sum(by_weighted[...] * weighted_row)
    shift = from_coarse[:coarse]
    weighted_shift = from_coarse[coarse : 2 * coarse]
    near_shift = from_coarse[2 * coarse : 2 * coarse + near]
    image = image_sum[...] - row_sum(cols[...] * near_shift)
    direction = state[0:1, :]
    state_out[1:2, :] = state[1:2, :] + step * direction
    state_out[2:3, :] = state[2:3, :] - step * image
    if not again:
        return
    near_turned = from_coarse[2 * coarse + near : 2 * coarse + 2 * near] + from_weighted[coarse : coarse + near]
    coeff_change = (
        from_coarse[2 * coarse + 2 * near :]
        + from_weighted[coarse + near :]
        + lane_sum(by_products[...] * totals)
    )
    found_weighted = from_weighted[:coarse]
    cross = totals[:, 37:38] - row_sum(shift * weighted[...])
    square = lane_sum(row_sum(gathered[:, LANES:])) - row_sum(shift * (2.0 * found_weighted - weighted_shift))
    rho_next = rho[...] - step * (2.0 * cross - step * square)
    weighted_out[...] = weighted[...] - step * (found_weighted - weighted_shift)
    rho_out[...] = rho_next
    change = weights[...] * image - row_sum(cols[...] * near_turned) - row_sum(basis[...] * coeff_change)
    deflated = state[3:4, :] - step * change
    state_out[3:4, :] = deflated
    state_out[0:1, :] = deflated + (rho_next / rho[...]) * direction


def apply(count, operator, held, arrived, state, tests, images, weights, live, product, sums):
    rows = held.shape[0] // PARTS
    direction = state[0:1, :]
    rounded = jnp.broadcast_to(direction, (16, direction.shape[1])).astype(jnp.bfloat16)
    total = None
    for part in range(PARTS):
        pltpu.make_async_copy(
            operator.at[pl.ds(part * rows, rows)], held.at[pl.ds(part * rows, rows)], arrived.at[part]
        ).wait()
        piece = jnp.dot(
            rounded[:, part * rows : (part + 1) * rows],
            held[part * rows : (part + 1) * rows, :],
            preferred_element_type=jnp.float32,
        )
        total = piece if total is None else total + piece
    found = live[...] * total[0:1, :]
    product[...] = found
    column = jnp.concatenate([lane_sum(tests[...] * found), lane_sum(images[...] * found)], axis=0)
    size = column.shape[0]
    rows_of = lax.broadcasted_iota(jnp.int32, (size, LANES), 0)
    lanes_of = lax.broadcasted_iota(jnp.int32, (size, LANES), 1)
    lane = lax.broadcasted_iota(jnp.int32, (1, LANES), 1)
    row = row_sum(jnp.where(rows_of == lanes_of, column, 0.0))
    row = row + jnp.where(lane == 36, lane_sum(direction * found), 0.0)
    sums[...] = row + jnp.where(lane == 37, lane_sum(weights[...] * state[2:3, :] * found), 0.0)


def fetch(operator, held, arrived):
    rows = held.shape[0] // PARTS
    for part in range(PARTS):
        pltpu.make_async_copy(
            operator.at[pl.ds(part * rows, rows)], held.at[pl.ds(part * rows, rows)], arrived.at[part]
        ).start()


def step_kernel(count, again, *refs):
    if not again:
        gathered, image_sum, state, weighted, rho, *rest = refs
        advance(count, gathered, image_sum, state, rest[-1], weighted, rho, None, None, rest[:-1], False)
        return
    gathered, image_sum, state, weighted, rho = refs[:5]
    shared = refs[5:13]
    operator, tests, images, live = refs[13:17]
    state_out, weighted_out, rho_out, product, sums, held, arrived = refs[17:]
    fetch(operator, held, arrived)
    advance(count, gathered, image_sum, state, state_out, weighted, rho, weighted_out, rho_out, shared, True)
    apply(count, operator, held, arrived, state_out, tests, images, shared[-1], live, product, sums)


def first_kernel(count, state, operator, tests, images, weights, live, product, sums, held, arrived):
    fetch(operator, held, arrived)
    apply(count, operator, held, arrived, state, tests, images, weights, live, product, sums)


def shape_of(*dims):
    return jax.ShapeDtypeStruct(dims, jnp.float32)


def local(dual_ops, neighbors, face_counts, load_terms, precond_terms, rigid_terms, recycled_terms):
    local_op = dual_ops[0, 0]
    neighbor_ids = neighbors[0, 0]
    load = load_terms[0, 0]
    rigid = rigid_terms[0, 0]
    recycled = recycled_terms[0, 0].astype(jnp.float32)
    clusters = lax.axis_size("clu")
    members = lax.axis_size("sub")
    clu_index = lax.axis_index("clu")
    sub_index = lax.axis_index("sub")
    slots = load.shape[-1]
    width = 6 * slots
    count = recycled.shape[0]
    per = count // members
    piece = 4 * per * slots
    coarse = 6 * clusters
    onehot = (neighbor_ids[:, None] == jnp.arange(members, dtype=jnp.int32)[None, :]).astype(
        jnp.float32
    )
    live = (
        jnp.arange(slots, dtype=jnp.int32)[None, :] < face_counts[0, 0][:, None]
    ).astype(jnp.float32)
    flat_live = live.reshape(1, width)

    targets = jnp.arange(coarse, dtype=jnp.int32)[:, None]
    sources = jnp.arange(18 * clusters, dtype=jnp.int32)[None, :]
    spread = (
        targets == 6 * (sources // 18) + (sources % 18) - 6
    ).astype(jnp.float32)
    spread_back = spread.T.reshape(clusters, 18, coarse)

    def nearby(values):
        padded = jnp.pad(values, ((6, 6), (0, 0)))
        return lax.dynamic_slice_in_dim(padded, 6 * clu_index, 18, 0)

    def to_carriers(values):
        faces = values.reshape(members, per, 6, slots)[:, :, :4]
        return faces.transpose(0, 2, 1, 3).reshape(members, piece)

    def from_carriers(received):
        faces = received.reshape(members, 4, per, slots).transpose(0, 2, 1, 3)
        return faces.reshape(count, 4, slots)

    few = jnp.concatenate([load[None], precond_terms[0, 0][None], rigid], axis=0)
    few_count = few.shape[0]
    low, high = rims(jnp.concatenate([few, recycled], axis=0))
    direct = dot(onehot.T, few[:, :4].transpose(1, 0, 2).reshape(4, few_count * slots))
    ids = jnp.broadcast_to(padded_row(neighbor_ids.astype(jnp.float32))[None], (members, LANES))
    received = trade(jnp.concatenate([to_carriers(recycled), direct, ids], axis=1), "sub")
    table = received[:, piece + few_count * slots :][:, :4]
    slots_of = 4 * members
    row_member = (lax.broadcasted_iota(jnp.int32, (slots_of, slots_of), 0) // 4).astype(jnp.float32)
    lane_member = (lax.broadcasted_iota(jnp.int32, (slots_of, slots_of), 1) // 4).astype(jnp.float32)
    route = jnp.where(
        (table.reshape(slots_of, 1) == lane_member) & (table.reshape(1, slots_of) == row_member), 1.0, 0.0
    )

    def carry(arrived):
        return dot(route, arrived.reshape(4 * members, per * slots)).reshape(members, piece)

    few_inner = dot(onehot, received[:, piece : piece + few_count * slots])
    few_inner = few_inner.reshape(4, few_count, slots).transpose(1, 0, 2)
    few_copy = six_faces(few_inner, low[:few_count], high[:few_count])
    demand = (live * (load + few_copy[0])).reshape(1, width)
    weights = (0.5 * live * (few[1] + few_copy[1])).reshape(1, width)
    face_index = jnp.arange(6, dtype=jnp.int32)
    inner_face = (face_index < 4).astype(jnp.float32)[:, None]
    below_face = (face_index == 4).astype(jnp.float32)[:, None]
    above_face = (face_index == 5).astype(jnp.float32)[:, None]
    rigid_copy = few_copy[2:]
    cols = jnp.concatenate(
        [
            live * rigid_copy * below_face,
            live * (rigid + rigid_copy * inner_face),
            live * rigid_copy * above_face,
        ],
        axis=0,
    ).reshape(18, width)
    weighted_cols = weights * cols
    flat_recycled = recycled.reshape(count, width)
    sums = dot_t(
        cols,
        jnp.concatenate(
            [0.5 * cols, 0.5 * weighted_cols, flat_recycled, load.reshape(1, width)], axis=0
        ),
    )
    sums_size = sums.size
    sums_row = padded_row(sums)
    received = trade(
        jnp.concatenate(
            [carry(received[:, :piece]), jnp.broadcast_to(sums_row[None], (members, sums_row.shape[0]))],
            axis=1,
        ),
        "sub",
    )
    basis_raw = (
        live * (recycled + six_faces(from_carriers(received[:, :piece]), low[few_count:], high[few_count:]))
    ).reshape(count, width)
    gathered = everyone(jnp.sum(received[:, piece:], axis=0), "clu")
    gathered = gathered[:, :sums_size].reshape(clusters, 18, 37 + count)
    pairs = jnp.einsum(
        "cgab,cbx->cagx",
        jnp.stack([gathered[:, :, :18], gathered[:, :, 18:36]], axis=1),
        spread_back,
        precision=precise,
    ).reshape(18 * clusters, 2 * coarse)
    assembled = dot(
        spread,
        jnp.concatenate([pairs, gathered[:, :, 36:].reshape(18 * clusters, count + 1)], axis=1),
    )
    coarse_inverse = spd_inverse(assembled[:, :coarse])
    weighted_matrix = assembled[:, coarse : 2 * coarse]
    amounts = nearby(dot(coarse_inverse, assembled[:, 2 * coarse :]))
    projected = jnp.concatenate([basis_raw, demand], axis=0) - dot(amounts.T, cols)
    basis = projected[:count]
    start = projected[count:]

    products = flat_live * jnp.dot(
        basis.astype(jnp.bfloat16), local_op, preferred_element_type=jnp.float32
    )
    low, high = rims(products.reshape(count, 6, slots))
    both_cols = jnp.concatenate([cols, weighted_cols], axis=0)
    grouped = both_cols.reshape(2, 3, 6, width).transpose(0, 2, 1, 3).reshape(12, 3, width)
    grouped = jnp.pad(grouped, ((0, 0), (0, 1), (0, 0))).reshape(48, width)
    tests = jnp.concatenate([basis, grouped], axis=0)
    sums = dot_t(tests, products)
    start_row = dot_t(0.5 * start, tests)
    basis_parts = count // 4
    shares = jnp.concatenate(
        [
            sums.reshape(basis_parts + 12, 4 * count),
            jnp.pad(start_row[:, :count], ((0, 0), (0, 3 * count))),
            jnp.pad(start_row[:, count:], ((0, 0), (0, 4 * count - 48))),
            jnp.zeros((members - basis_parts - 14, 4 * count), jnp.float32),
        ],
        axis=0,
    )
    received = trade(
        jnp.concatenate([to_carriers(products), shares], axis=1), "sub"
    )
    share = everyone(jnp.sum(received[:, piece:], axis=0), "clu").reshape(clusters, 4, count)
    whole = jnp.pad(jnp.sum(share, axis=0), ((0, clusters - 4), (0, 0)))
    beside = jnp.pad(share[:, :3], ((1, 1), (0, 0), (0, 0)))
    shifted = beside[2:, 0] + beside[1:-1, 1] + beside[:-2, 2]
    is_coarse = (sub_index >= basis_parts) & (sub_index < basis_parts + 12)
    is_listed = sub_index == basis_parts + 13
    share = jnp.where(is_coarse, shifted, jnp.where(is_listed, share[:, 0], whole))
    share_size = clusters * count
    received = trade(
        jnp.concatenate(
            [
                carry(received[:, :piece]),
                jnp.broadcast_to(share.reshape(1, share_size), (members, share_size)),
            ],
            axis=1,
        ),
        "sub",
    )
    images = (
        live
        * (products.reshape(count, 6, slots) + six_faces(from_carriers(received[:, :piece]), low, high))
    ).reshape(count, width)
    parts = received[:, piece:].reshape(members, clusters, count)
    energy_raw = parts[:basis_parts, :4].reshape(count, count)
    image_coarse = parts[basis_parts : basis_parts + 6].transpose(1, 0, 2).reshape(coarse, count)
    image_weighted = parts[basis_parts + 6 : basis_parts + 12].transpose(1, 0, 2).reshape(coarse, count)
    start_sums = parts[basis_parts + 12, 0][:, None]
    listed = parts[basis_parts + 13, :, 24:48].reshape(clusters, 6, 4)[:, :, :3]
    start_weighted = dot(spread, listed.transpose(0, 2, 1).reshape(18 * clusters, 1))
    energy_inverse = spd_inverse(0.5 * (energy_raw + energy_raw.T))
    amount = dot(energy_inverse, start_sums)

    mixed = dot(amount.T, jnp.concatenate([basis, images], axis=1))
    solution = mixed[:, :width]
    shift = dot(coarse_inverse, dot(image_coarse, amount))
    residual = start - mixed[:, width:] + dot(nearby(shift).T, cols)
    weighted_residual = start_weighted - dot(image_weighted, amount) + dot(weighted_matrix, shift)
    amounts = dot(coarse_inverse, weighted_residual)
    search = weights * residual - dot(nearby(amounts).T, cols)
    weighted_images = weights * images
    near_rows = lax.broadcasted_iota(jnp.int32, (24, coarse), 0)
    near_lanes = lax.broadcasted_iota(jnp.int32, (24, coarse), 1)
    near_select = ((near_lanes == 6 * clu_index + near_rows - 6) & (near_rows < 18)).astype(jnp.float32)
    weighted_inverse = dot(weighted_matrix, coarse_inverse)
    twice = dot(coarse_inverse, weighted_inverse)
    both_near = dot(near_select, jnp.concatenate([coarse_inverse, twice], axis=1))
    by_shift = dot(energy_inverse, image_weighted.T)
    by_amounts = dot(energy_inverse, image_coarse.T)
    weighted_coeff = -dot(by_amounts, coarse_inverse)
    coarse_coeff = dot(by_amounts, twice) - dot(by_shift, coarse_inverse)
    lane_pad = ((0, 0), (0, LANES - coarse))
    by_coarse = jnp.pad(
        jnp.concatenate(
            [coarse_inverse, weighted_inverse, both_near[:, :coarse], -both_near[:, coarse:], coarse_coeff],
            axis=0,
        ),
        lane_pad,
    )
    by_weighted = jnp.pad(
        jnp.concatenate(
            [jnp.eye(coarse, dtype=jnp.float32), both_near[:, :coarse], weighted_coeff], axis=0
        ),
        lane_pad,
    )
    by_products = jnp.pad(energy_inverse, ((0, 0), (40, LANES - 40 - count)))
    lift_rows = lax.broadcasted_iota(jnp.int32, (LANES, 6 * LANES), 0)
    lift_lanes = lax.broadcasted_iota(jnp.int32, (LANES, 6 * LANES), 1)
    lift = (
        (lift_rows // 6 == lift_lanes // LANES) & (lift_rows % 6 == (lift_lanes % LANES) % 6)
    ).astype(jnp.bfloat16)
    mask_rows = lax.broadcasted_iota(jnp.int32, (clusters, 6 * LANES), 0)
    mask_lanes = lax.broadcasted_iota(jnp.int32, (clusters, 6 * LANES), 1)
    lift_mask = (
        mask_rows + (mask_lanes // LANES) % 3 - 1 == (mask_lanes % LANES) // 6
    ).astype(jnp.float32)
    padded_cols = jnp.pad(cols, ((0, 6), (0, 0)))
    tests = jnp.pad(both_cols, ((0, 4), (0, 0)))

    sums_row = padded_row(
        dot_t(jnp.concatenate([products, 0.5 * residual], axis=0), weights * residual)
    )
    received = everyone(
        jnp.concatenate([sums_row, weights[0, : 4 * slots]]), "sub"
    )
    all_weights = received[:, LANES:].reshape(slots_of, slots)
    totals = jnp.sum(
        everyone(jnp.sum(received[:, :LANES], axis=0), "clu"), axis=0, keepdims=True
    )
    rho = totals[:, count : count + 1]
    coeff = dot(energy_inverse, totals[:, :count].T) - dot(by_amounts, amounts)
    deflated_search = search - dot(coeff.T, basis)
    state = jnp.concatenate([deflated_search, solution, residual, deflated_search], axis=0)
    shared = (lift, lift_mask, by_coarse, by_weighted, by_products, padded_cols, basis, weights)
    scratch = [pltpu.VMEM(local_op.shape, jnp.bfloat16), pltpu.SemaphoreType.DMA((PARTS,))]
    params = pltpu.CompilerParams(vmem_limit_bytes=24 * 2**20)
    anywhere = pl.BlockSpec(memory_space=pl.ANY)
    cost = pl.CostEstimate(
        flops=2 * width * width, bytes_accessed=2 * width * width + 4 * 300 * width, transcendentals=0
    )
    product, sums = pl.pallas_call(
        functools.partial(first_kernel, count),
        out_shape=(shape_of(1, width), shape_of(1, LANES)),
        in_specs=[VMEM, anywhere, VMEM, VMEM, VMEM, VMEM],
        out_specs=(VMEM, VMEM),
        scratch_shapes=scratch,
        compiler_params=params,
        cost_estimate=cost,
    )(state, local_op, tests, weighted_images, weights, flat_live)
    for iteration in range(ITERS):
        last = iteration + 1 == ITERS
        faces = product.reshape(6, slots)
        low, high = rims(faces[None])
        sent = [product[0, : 4 * slots], sums[0]]
        if not last:
            beside = jnp.concatenate([jnp.zeros((1, 4 * slots), jnp.float32), low, high], axis=1)
            square = weights * product * (product + beside)
            sent.append(jnp.sum(square.reshape(width // LANES, LANES), axis=0))
        received = everyone(jnp.concatenate(sent), "sub")
        all_faces = received[:, : 4 * slots].reshape(slots_of, slots)
        all_partners = dot(route, all_faces)
        inner = lax.dynamic_slice_in_dim(all_partners, 4 * sub_index, 4, 0)
        assembled = (live * (faces + jnp.concatenate([inner, low, high], axis=0))).reshape(1, width)
        sums = jnp.sum(received[:, 4 * slots :], axis=0)
        if not last:
            cross = jnp.sum(all_weights * all_faces * all_partners, axis=0)
            cross = jnp.sum(cross.reshape(slots // LANES, LANES), axis=0)
            sums = sums + jnp.concatenate([jnp.zeros((LANES,), jnp.float32), cross])
        gathered = everyone(sums, "clu")
        ahead = (gathered, assembled, state, weighted_residual, rho)
        if last:
            state = pl.pallas_call(
                functools.partial(step_kernel, count, False),
                out_shape=shape_of(4, width),
                in_specs=[VMEM] * 13,
                out_specs=VMEM,
                compiler_params=params,
            )(*ahead, *shared)
            break
        state, weighted_residual, rho, product, sums = pl.pallas_call(
            functools.partial(step_kernel, count, True),
            out_shape=(
                shape_of(4, width),
                shape_of(coarse, 1),
                shape_of(1, 1),
                shape_of(1, width),
                shape_of(1, LANES),
            ),
            in_specs=[VMEM] * 13 + [anywhere, VMEM, VMEM, VMEM],
            out_specs=(VMEM,) * 5,
            scratch_shapes=scratch,
            compiler_params=params,
            cost_estimate=cost,
        )(*ahead, *shared, local_op, tests, weighted_images, flat_live)
    solution, residual = state[1], state[2]
    return (solution.reshape(1, 1, 6, slots), residual.reshape(1, 1, 6, slots))


def solution(mesh):
    return jax.shard_map(
        local,
        mesh=mesh,
        in_specs=(
            P("clu", "sub", None, None),
            P("clu", "sub", None),
            P("clu", "sub", None),
            P("clu", "sub", None, None),
            P("clu", "sub", None, None),
            P("clu", "sub", None, None, None),
            P("clu", "sub", None, None, None),
        ),
        out_specs=(P("clu", "sub", None, None), P("clu", "sub", None, None)),
        check_vma=False,
    )
```

```python
import functools

import jax
import jax.numpy as jnp
from jax import lax
from jax.experimental import pallas as pl
from jax.experimental.pallas import tpu as pltpu
from jax.sharding import PartitionSpec as P

ITERS = 3
LANES = 128


precise = lax.Precision.HIGHEST


def dot(first, second):
    return jnp.dot(first, second, precision=precise, preferred_element_type=jnp.float32)


def dot_t(first, second):
    return lax.dot_general(
        first, second, (((1,), (1,)), ((), ())), precision=precise, preferred_element_type=jnp.float32
    )


def padded_row(values, multiple=LANES):
    flat = values.reshape(-1)
    return jnp.pad(flat, (0, -flat.shape[0] % multiple))


def everyone(row, axis):
    count = lax.axis_size(axis)
    sent = jnp.broadcast_to(row[None, None, :], (count, 1, row.shape[0]))
    return lax.all_to_all(sent, axis, split_axis=0, concat_axis=0, tiled=True)[:, 0, :]


def trade(rows, axis):
    return lax.all_to_all(rows[:, None, :], axis, split_axis=0, concat_axis=0, tiled=True)[:, 0, :]


def rims(values):
    count = lax.axis_size("clu")
    forward = [(i, i + 1) for i in range(count - 1)]
    backward = [(i + 1, i) for i in range(count - 1)]
    low = lax.ppermute(values[:, 5, :], "clu", forward)
    high = lax.ppermute(values[:, 4, :], "clu", backward)
    return low, high


def six_faces(inner, low, high):
    return jnp.concatenate([inner, low[:, None, :], high[:, None, :]], axis=1)


def invert(matrix_ref, inverse_ref):
    size = matrix_ref.shape[0]
    lane = lax.broadcasted_iota(jnp.int32, (8, size), 1)
    row = lax.broadcasted_iota(jnp.int32, (8, 1), 0)
    tiles = [matrix_ref[8 * t : 8 * t + 8, :] for t in range(size // 8)]
    for k in range(0, size, 2):
        home, at = divmod(k, 8)

        def spread_out(values, place):
            return jnp.broadcast_to(values[:, place : place + 1], (8, size))

        first = jnp.broadcast_to(tiles[home][at : at + 1, :], (8, size))
        second = jnp.broadcast_to(tiles[home][at + 1 : at + 2, :], (8, size))
        across = spread_out(second, k)
        first_part = 1.0 / spread_out(first, k)
        ratio = across * first_part
        second_part = 1.0 / (spread_out(second, k + 1) - ratio * across)
        mixed_part = ratio * second_part
        here, after = lane == k, lane == k + 1
        either = here | after
        first = jnp.where(either, jnp.where(here, 1.0, 0.0), first)
        second = jnp.where(either, jnp.where(after, 1.0, 0.0), second)
        first_scaled = (first_part + ratio * mixed_part) * first - mixed_part * second
        second_scaled = second_part * second - mixed_part * first
        for t, tile in enumerate(tiles):
            first_column, second_column = tile[:, k : k + 1], tile[:, k + 1 : k + 2]
            kept = jnp.where(either, 0.0, tile)
            if t == home:
                pivots = (row == at) | (row == at + 1)
                first_column = jnp.where(pivots, jnp.where(row == at, -1.0, 0.0), first_column)
                second_column = jnp.where(pivots, jnp.where(row == at + 1, -1.0, 0.0), second_column)
                kept = jnp.where(pivots, 0.0, kept)
            tiles[t] = kept - first_column * first_scaled - second_column * second_scaled
    for t, tile in enumerate(tiles):
        inverse_ref[8 * t : 8 * t + 8, :] = tile


def spd_inverse(matrix):
    size = matrix.shape[0]
    return pl.pallas_call(
        invert,
        out_shape=jax.ShapeDtypeStruct((size, size), jnp.float32),
        in_specs=[pl.BlockSpec(memory_space=pltpu.VMEM)],
        out_specs=pl.BlockSpec(memory_space=pltpu.VMEM),
        cost_estimate=pl.CostEstimate(flops=2 * size**3, bytes_accessed=8 * size**2, transcendentals=size),
    )(matrix)


PARTS = 4
VMEM = pl.BlockSpec(memory_space=pltpu.VMEM)


def lane_sum(values):
    return jnp.sum(values, axis=1, keepdims=True)


def row_sum(values):
    return jnp.sum(values, axis=0, keepdims=True)


def advance(count, gathered, image_sum, state, state_out, weighted, rho, weighted_out, rho_out, refs, again):
    spread, mask, by_coarse, by_weighted, by_products, cols, basis, weights = refs
    coarse = weighted.shape[0]
    near = cols.shape[0]
    values = gathered[:, :LANES]
    high = values.astype(jnp.bfloat16)
    rest = values - high.astype(jnp.float32)
    middle = rest.astype(jnp.bfloat16)
    low = (rest - middle.astype(jnp.float32)).astype(jnp.bfloat16)
    lifted = (
        jnp.dot(high, spread[...], preferred_element_type=jnp.float32)
        + jnp.dot(middle, spread[...], preferred_element_type=jnp.float32)
        + jnp.dot(low, spread[...], preferred_element_type=jnp.float32)
    )
    lifted = row_sum(lifted * mask[...])
    coarse_row = lifted[:, :LANES] + lifted[:, LANES : 2 * LANES] + lifted[:, 2 * LANES : 3 * LANES]
    weighted_row = (
        lifted[:, 3 * LANES : 4 * LANES] + lifted[:, 4 * LANES : 5 * LANES] + lifted[:, 5 * LANES :]
    )
    totals = row_sum(values)
    rho_now = rho[:, count : count + 1]
    step = rho_now / totals[:, 36:37]
    from_coarse = lane_sum(by_coarse[...] * coarse_row)
    from_weighted = lane_sum(by_weighted[...] * weighted_row)
    shift = from_coarse[:coarse]
    weighted_shift = from_coarse[coarse : 2 * coarse]
    near_shift = from_coarse[2 * coarse : 2 * coarse + near]
    image = image_sum[...] - row_sum(cols[...] * near_shift)
    direction = state[0:1, :]
    solution = state[1:2, :] + step * direction
    residual = state[2:3, :] - step * image
    if not again:
        state_out[0][...] = solution
        state_out[1][...] = residual
        return
    state_out[1:2, :] = solution
    state_out[2:3, :] = residual
    near_turned = from_coarse[2 * coarse + near : 2 * coarse + 2 * near] + from_weighted[coarse : coarse + near]
    coeff_change = (
        from_coarse[2 * coarse + 2 * near :]
        + from_weighted[coarse + near :]
        + lane_sum(by_products[...] * totals)
    )
    found_weighted = from_weighted[:coarse]
    cross = totals[:, 37:38] - row_sum(shift * weighted[...])
    square = lane_sum(row_sum(gathered[:, LANES:])) - row_sum(shift * (2.0 * found_weighted - weighted_shift))
    rho_next = rho_now - step * (2.0 * cross - step * square)
    weighted_out[...] = weighted[...] - step * (found_weighted - weighted_shift)
    rho_out[...] = jnp.broadcast_to(rho_next, rho_out.shape)
    change = weights[...] * image - row_sum(cols[...] * near_turned) - row_sum(basis[...] * coeff_change)
    deflated = state[3:4, :] - step * change
    state_out[3:4, :] = deflated
    state_out[0:1, :] = deflated + (rho_next / rho_now) * direction


def apply(count, operator, held, arrived, state, tests, images, weights, live, product, sums):
    rows = held.shape[0] // PARTS
    direction = state[0:1, :]
    rounded = jnp.broadcast_to(direction, (16, direction.shape[1])).astype(jnp.bfloat16)
    total = None
    for part in range(PARTS):
        pltpu.make_async_copy(
            operator.at[pl.ds(part * rows, rows)], held.at[pl.ds(part * rows, rows)], arrived.at[part]
        ).wait()
        piece = jnp.dot(
            rounded[:, part * rows : (part + 1) * rows],
            held[part * rows : (part + 1) * rows, :],
            preferred_element_type=jnp.float32,
        )
        total = piece if total is None else total + piece
    found = live[...] * total[0:1, :]
    product[...] = found
    column = jnp.concatenate([lane_sum(tests[...] * found), lane_sum(images[...] * found)], axis=0)
    size = column.shape[0]
    rows_of = lax.broadcasted_iota(jnp.int32, (size, LANES), 0)
    lanes_of = lax.broadcasted_iota(jnp.int32, (size, LANES), 1)
    lane = lax.broadcasted_iota(jnp.int32, (1, LANES), 1)
    row = row_sum(jnp.where(rows_of == lanes_of, column, 0.0))
    row = row + jnp.where(lane == 36, lane_sum(direction * found), 0.0)
    sums[...] = row + jnp.where(lane == 37, lane_sum(weights[...] * state[2:3, :] * found), 0.0)


def fetch(operator, held, arrived):
    rows = held.shape[0] // PARTS
    for part in range(PARTS):
        pltpu.make_async_copy(
            operator.at[pl.ds(part * rows, rows)], held.at[pl.ds(part * rows, rows)], arrived.at[part]
        ).start()


def step_kernel(count, again, *refs):
    if not again:
        gathered, image_sum, state, weighted, rho, *rest = refs
        outs = rest[-2:]
        advance(count, gathered, image_sum, state, outs, weighted, rho, None, None, rest[:-2], False)
        return
    gathered, image_sum, state, weighted, rho = refs[:5]
    shared = refs[5:13]
    operator, tests, images, live = refs[13:17]
    state_out, weighted_out, rho_out, product, sums, held, arrived = refs[17:]
    fetch(operator, held, arrived)
    advance(count, gathered, image_sum, state, state_out, weighted, rho, weighted_out, rho_out, shared, True)
    apply(count, operator, held, arrived, state_out, tests, images, shared[-1], live, product, sums)


def first_kernel(count, state, operator, tests, images, weights, live, product, sums, held, arrived):
    fetch(operator, held, arrived)
    apply(count, operator, held, arrived, state, tests, images, weights, live, product, sums)


def shape_of(*dims):
    return jax.ShapeDtypeStruct(dims, jnp.float32)


def local(dual_ops, neighbors, face_counts, load_terms, precond_terms, rigid_terms, recycled_terms):
    local_op = dual_ops[0, 0]
    neighbor_ids = neighbors[0, 0]
    load = load_terms[0, 0]
    rigid = rigid_terms[0, 0]
    recycled = recycled_terms[0, 0].astype(jnp.float32)
    clusters = lax.axis_size("clu")
    members = lax.axis_size("sub")
    clu_index = lax.axis_index("clu")
    sub_index = lax.axis_index("sub")
    slots = load.shape[-1]
    width = 6 * slots
    count = recycled.shape[0]
    per = count // members
    piece = 4 * per * slots
    coarse = 6 * clusters
    onehot = (neighbor_ids[:, None] == jnp.arange(members, dtype=jnp.int32)[None, :]).astype(
        jnp.float32
    )
    live = (
        jnp.arange(slots, dtype=jnp.int32)[None, :] < face_counts[0, 0][:, None]
    ).astype(jnp.float32)
    flat_live = live.reshape(1, width)

    targets = jnp.arange(coarse, dtype=jnp.int32)[:, None]
    sources = jnp.arange(18 * clusters, dtype=jnp.int32)[None, :]
    spread = (
        targets == 6 * (sources // 18) + (sources % 18) - 6
    ).astype(jnp.float32)
    spread_back = spread.T.reshape(clusters, 18, coarse)

    def nearby(values):
        padded = jnp.pad(values, ((6, 6), (0, 0)))
        return lax.dynamic_slice_in_dim(padded, 6 * clu_index, 18, 0)

    def to_carriers(values):
        faces = values.reshape(members, per, 6, slots)[:, :, :4]
        return faces.transpose(0, 2, 1, 3).reshape(members, piece)

    def from_carriers(received):
        faces = received.reshape(members, 4, per, slots).transpose(0, 2, 1, 3)
        return faces.reshape(count, 4, slots)

    few = jnp.concatenate([load[None], precond_terms[0, 0][None], rigid], axis=0)
    few_count = few.shape[0]
    direct = dot(onehot.T, few[:, :4].transpose(1, 0, 2).reshape(4, few_count * slots))
    ids = jnp.broadcast_to(padded_row(neighbor_ids.astype(jnp.float32))[None], (members, LANES))
    first_blocks = jnp.concatenate([to_carriers(recycled), direct, ids], axis=1)
    few_later, first_blocks = lax.optimization_barrier((few, first_blocks))
    received = trade(first_blocks, "sub")
    few_low, few_high = rims(few_later)
    table = received[:, piece + few_count * slots :][:, :4]
    slots_of = 4 * members
    row_member = (lax.broadcasted_iota(jnp.int32, (slots_of, slots_of), 0) // 4).astype(jnp.float32)
    lane_member = (lax.broadcasted_iota(jnp.int32, (slots_of, slots_of), 1) // 4).astype(jnp.float32)
    route = jnp.where(
        (table.reshape(slots_of, 1) == lane_member) & (table.reshape(1, slots_of) == row_member), 1.0, 0.0
    )

    def carry(arrived):
        return dot(route, arrived.reshape(4 * members, per * slots)).reshape(members, piece)

    few_inner = dot(onehot, received[:, piece : piece + few_count * slots])
    few_inner = few_inner.reshape(4, few_count, slots).transpose(1, 0, 2)
    few_copy = six_faces(few_inner, few_low, few_high)
    demand = (live * (load + few_copy[0])).reshape(1, width)
    weights = (0.5 * live * (few[1] + few_copy[1])).reshape(1, width)
    face_index = jnp.arange(6, dtype=jnp.int32)
    inner_face = (face_index < 4).astype(jnp.float32)[:, None]
    below_face = (face_index == 4).astype(jnp.float32)[:, None]
    above_face = (face_index == 5).astype(jnp.float32)[:, None]
    rigid_copy = few_copy[2:]
    cols = jnp.concatenate(
        [
            live * rigid_copy * below_face,
            live * (rigid + rigid_copy * inner_face),
            live * rigid_copy * above_face,
        ],
        axis=0,
    ).reshape(18, width)
    weighted_cols = weights * cols
    flat_recycled = recycled.reshape(count, width)
    sums = dot_t(
        cols,
        jnp.concatenate(
            [0.5 * cols, 0.5 * weighted_cols, flat_recycled, load.reshape(1, width)], axis=0
        ),
    )
    sums_size = sums.size
    sums_row = padded_row(sums)
    second_blocks = jnp.concatenate(
        [carry(received[:, :piece]), jnp.broadcast_to(sums_row[None], (members, sums_row.shape[0]))],
        axis=1,
    )
    recycled_later, second_blocks = lax.optimization_barrier((recycled, second_blocks))
    received = trade(second_blocks, "sub")
    low, high = rims(recycled_later)
    basis_raw = (
        live * (recycled + six_faces(from_carriers(received[:, :piece]), low, high))
    ).reshape(count, width)
    gathered = everyone(jnp.sum(received[:, piece:], axis=0), "clu")
    gathered = gathered[:, :sums_size].reshape(clusters, 18, 37 + count)
    pairs = jnp.einsum(
        "cgab,cbx->cagx",
        jnp.stack([gathered[:, :, :18], gathered[:, :, 18:36]], axis=1),
        spread_back,
        precision=precise,
    ).reshape(18 * clusters, 2 * coarse)
    assembled = dot(
        spread,
        jnp.concatenate([pairs, gathered[:, :, 36:].reshape(18 * clusters, count + 1)], axis=1),
    )
    coarse_inverse = spd_inverse(assembled[:, :coarse])
    weighted_matrix = assembled[:, coarse : 2 * coarse]
    amounts = nearby(dot(coarse_inverse, assembled[:, 2 * coarse :]))
    projected = jnp.concatenate([basis_raw, demand], axis=0) - dot(amounts.T, cols)
    basis = projected[:count]
    start = projected[count:]

    products = flat_live * jnp.dot(
        basis.astype(jnp.bfloat16), local_op, preferred_element_type=jnp.float32
    )
    both_cols = jnp.concatenate([cols, weighted_cols], axis=0)
    grouped = both_cols.reshape(2, 3, 6, width).transpose(0, 2, 1, 3).reshape(12, 3, width)
    grouped = jnp.pad(grouped, ((0, 0), (0, 1), (0, 0))).reshape(48, width)
    tests = jnp.concatenate([basis, grouped], axis=0)
    sums = dot_t(tests, products)
    start_row = dot_t(0.5 * start, tests)
    basis_parts = count // 4
    shares = jnp.concatenate(
        [
            sums.reshape(basis_parts + 12, 4 * count),
            jnp.pad(start_row[:, :count], ((0, 0), (0, 3 * count))),
            jnp.pad(start_row[:, count:], ((0, 0), (0, 4 * count - 48))),
            jnp.zeros((members - basis_parts - 14, 4 * count), jnp.float32),
        ],
        axis=0,
    )
    blocks = jnp.concatenate([to_carriers(products), shares], axis=1)
    products_later, blocks = lax.optimization_barrier((products, blocks))
    received = trade(blocks, "sub")
    low, high = rims(products_later.reshape(count, 6, slots))
    share = everyone(jnp.sum(received[:, piece:], axis=0), "clu").reshape(clusters, 4, count)
    whole = jnp.pad(jnp.sum(share, axis=0), ((0, clusters - 4), (0, 0)))
    beside = jnp.pad(share[:, :3], ((1, 1), (0, 0), (0, 0)))
    shifted = beside[2:, 0] + beside[1:-1, 1] + beside[:-2, 2]
    is_coarse = (sub_index >= basis_parts) & (sub_index < basis_parts + 12)
    is_listed = sub_index == basis_parts + 13
    share = jnp.where(is_coarse, shifted, jnp.where(is_listed, share[:, 0], whole))
    share_size = clusters * count
    received = trade(
        jnp.concatenate(
            [
                carry(received[:, :piece]),
                jnp.broadcast_to(share.reshape(1, share_size), (members, share_size)),
            ],
            axis=1,
        ),
        "sub",
    )
    images = (
        live
        * (products.reshape(count, 6, slots) + six_faces(from_carriers(received[:, :piece]), low, high))
    ).reshape(count, width)
    parts = received[:, piece:].reshape(members, clusters, count)
    energy_raw = parts[:basis_parts, :4].reshape(count, count)
    image_coarse = parts[basis_parts : basis_parts + 6].transpose(1, 0, 2).reshape(coarse, count)
    image_weighted = parts[basis_parts + 6 : basis_parts + 12].transpose(1, 0, 2).reshape(coarse, count)
    start_sums = parts[basis_parts + 12, 0][:, None]
    listed = parts[basis_parts + 13, :, 24:48].reshape(clusters, 6, 4)[:, :, :3]
    start_weighted = dot(spread, listed.transpose(0, 2, 1).reshape(18 * clusters, 1))
    energy_inverse = spd_inverse(0.5 * (energy_raw + energy_raw.T))
    amount = dot(energy_inverse, start_sums)

    mixed = dot(amount.T, jnp.concatenate([basis, images], axis=1))
    solution = mixed[:, :width]
    shift = dot(coarse_inverse, dot(image_coarse, amount))
    residual = start - mixed[:, width:] + dot(nearby(shift).T, cols)
    weighted_residual = start_weighted - dot(image_weighted, amount) + dot(weighted_matrix, shift)
    amounts = dot(coarse_inverse, weighted_residual)
    search = weights * residual - dot(nearby(amounts).T, cols)
    weighted_images = weights * images
    sums_row = padded_row(
        dot_t(jnp.concatenate([products, 0.5 * residual], axis=0), weights * residual)
    )
    received = everyone(
        jnp.concatenate([sums_row, weights[0, : 4 * slots]]), "sub"
    )
    all_weights = received[:, LANES:].reshape(slots_of, slots)
    to_clusters = jnp.sum(received[:, :LANES], axis=0)
    totals = jnp.sum(everyone(to_clusters, "clu"), axis=0, keepdims=True)
    rho = totals
    (to_clusters, weighted_matrix, coarse_inverse, energy_inverse, image_weighted, image_coarse) = (
        lax.optimization_barrier(
            (to_clusters, weighted_matrix, coarse_inverse, energy_inverse, image_weighted, image_coarse)
        )
    )
    near_rows = lax.broadcasted_iota(jnp.int32, (24, coarse), 0)
    near_lanes = lax.broadcasted_iota(jnp.int32, (24, coarse), 1)
    near_select = ((near_lanes == 6 * clu_index + near_rows - 6) & (near_rows < 18)).astype(jnp.float32)
    weighted_inverse = dot(weighted_matrix, coarse_inverse)
    twice = dot(coarse_inverse, weighted_inverse)
    both_near = dot(near_select, jnp.concatenate([coarse_inverse, twice], axis=1))
    by_shift = dot(energy_inverse, image_weighted.T)
    by_amounts = dot(energy_inverse, image_coarse.T)
    weighted_coeff = -dot(by_amounts, coarse_inverse)
    coarse_coeff = dot(by_amounts, twice) - dot(by_shift, coarse_inverse)
    lane_pad = ((0, 0), (0, LANES - coarse))
    by_coarse = jnp.pad(
        jnp.concatenate(
            [coarse_inverse, weighted_inverse, both_near[:, :coarse], -both_near[:, coarse:], coarse_coeff],
            axis=0,
        ),
        lane_pad,
    )
    by_weighted = jnp.pad(
        jnp.concatenate(
            [jnp.eye(coarse, dtype=jnp.float32), both_near[:, :coarse], weighted_coeff], axis=0
        ),
        lane_pad,
    )
    by_products = jnp.pad(energy_inverse, ((0, 0), (40, LANES - 40 - count)))
    lift_rows = lax.broadcasted_iota(jnp.int32, (LANES, 6 * LANES), 0)
    lift_lanes = lax.broadcasted_iota(jnp.int32, (LANES, 6 * LANES), 1)
    lift = (
        (lift_rows // 6 == lift_lanes // LANES) & (lift_rows % 6 == (lift_lanes % LANES) % 6)
    ).astype(jnp.bfloat16)
    mask_rows = lax.broadcasted_iota(jnp.int32, (clusters, 6 * LANES), 0)
    mask_lanes = lax.broadcasted_iota(jnp.int32, (clusters, 6 * LANES), 1)
    lift_mask = (
        mask_rows + (mask_lanes // LANES) % 3 - 1 == (mask_lanes % LANES) // 6
    ).astype(jnp.float32)
    padded_cols = jnp.pad(cols, ((0, 6), (0, 0)))
    tests = jnp.pad(both_cols, ((0, 4), (0, 0)))

    coeff = dot(energy_inverse, totals[:, :count].T) - dot(by_amounts, amounts)
    deflated_search = search - dot(coeff.T, basis)
    state = jnp.concatenate([deflated_search, solution, residual, deflated_search], axis=0)
    shared = (lift, lift_mask, by_coarse, by_weighted, by_products, padded_cols, basis, weights)
    scratch = [pltpu.VMEM(local_op.shape, jnp.bfloat16), pltpu.SemaphoreType.DMA((PARTS,))]
    anywhere = pl.BlockSpec(memory_space=pl.ANY)
    cost = pl.CostEstimate(
        flops=2 * width * width, bytes_accessed=2 * width * width + 4 * 300 * width, transcendentals=0
    )
    product, sums = pl.pallas_call(
        functools.partial(first_kernel, count),
        out_shape=(shape_of(1, width), shape_of(1, LANES)),
        in_specs=[VMEM, anywhere, VMEM, VMEM, VMEM, VMEM],
        out_specs=(VMEM, VMEM),
        scratch_shapes=scratch,
        cost_estimate=cost,
    )(state, local_op, tests, weighted_images, weights, flat_live)
    for iteration in range(ITERS):
        last = iteration + 1 == ITERS
        faces = product.reshape(6, slots)
        low, high = rims(faces[None])
        sent = [product[0, : 4 * slots], sums[0]]
        if not last:
            beside = jnp.concatenate([jnp.zeros((1, 4 * slots), jnp.float32), low, high], axis=1)
            square = weights * product * (product + beside)
            sent.append(jnp.sum(square.reshape(width // LANES, LANES), axis=0))
        received = everyone(jnp.concatenate(sent), "sub")
        all_faces = received[:, : 4 * slots].reshape(slots_of, slots)
        all_partners = dot(route, all_faces)
        inner = lax.dynamic_slice_in_dim(all_partners, 4 * sub_index, 4, 0)
        assembled = (live * (faces + jnp.concatenate([inner, low, high], axis=0))).reshape(1, width)
        sums = jnp.sum(received[:, 4 * slots :], axis=0)
        if not last:
            cross = jnp.sum(all_weights * all_faces * all_partners, axis=0)
            cross = jnp.sum(cross.reshape(slots // LANES, LANES), axis=0)
            sums = sums + jnp.concatenate([jnp.zeros((LANES,), jnp.float32), cross])
        gathered = everyone(sums, "clu")
        ahead = (gathered, assembled, state, weighted_residual, rho)
        if last:
            solution, residual = pl.pallas_call(
                functools.partial(step_kernel, count, False),
                out_shape=(shape_of(1, width), shape_of(1, width)),
                in_specs=[VMEM] * 13,
                out_specs=(VMEM, VMEM),
            )(*ahead, *shared)
            break
        state, weighted_residual, rho, product, sums = pl.pallas_call(
            functools.partial(step_kernel, count, True),
            out_shape=(
                shape_of(4, width),
                shape_of(coarse, 1),
                shape_of(1, LANES),
                shape_of(1, width),
                shape_of(1, LANES),
            ),
            in_specs=[VMEM] * 13 + [anywhere, VMEM, VMEM, VMEM],
            out_specs=(VMEM,) * 5,
            scratch_shapes=scratch,
            cost_estimate=cost,
        )(*ahead, *shared, local_op, tests, weighted_images, flat_live)
    return (solution.reshape(1, 1, 6, slots), residual.reshape(1, 1, 6, slots))


def solution(mesh):
    return jax.shard_map(
        local,
        mesh=mesh,
        in_specs=(
            P("clu", "sub", None, None),
            P("clu", "sub", None),
            P("clu", "sub", None),
            P("clu", "sub", None, None),
            P("clu", "sub", None, None),
            P("clu", "sub", None, None, None),
            P("clu", "sub", None, None, None),
        ),
        out_specs=(P("clu", "sub", None, None), P("clu", "sub", None, None)),
        check_vma=False,
    )
```

```python
import functools

import jax
import jax.numpy as jnp
from jax import lax
from jax.experimental import pallas as pl
from jax.experimental.pallas import tpu as pltpu
from jax.sharding import PartitionSpec as P

ITERS = 3
LANES = 128


precise = lax.Precision.HIGHEST


def dot(first, second):
    return jnp.dot(first, second, precision=precise, preferred_element_type=jnp.float32)


def dot_t(first, second):
    return lax.dot_general(
        first, second, (((1,), (1,)), ((), ())), precision=precise, preferred_element_type=jnp.float32
    )


def padded_row(values, multiple=LANES):
    flat = values.reshape(-1)
    return jnp.pad(flat, (0, -flat.shape[0] % multiple))


def everyone(row, axis):
    count = lax.axis_size(axis)
    sent = jnp.broadcast_to(row[None, None, :], (count, 1, row.shape[0]))
    return lax.all_to_all(sent, axis, split_axis=0, concat_axis=0, tiled=True)[:, 0, :]


def trade(rows, axis):
    return lax.all_to_all(rows[:, None, :], axis, split_axis=0, concat_axis=0, tiled=True)[:, 0, :]


def rims(values):
    count = lax.axis_size("clu")
    forward = [(i, i + 1) for i in range(count - 1)]
    backward = [(i + 1, i) for i in range(count - 1)]
    low = lax.ppermute(values[:, 5, :], "clu", forward)
    high = lax.ppermute(values[:, 4, :], "clu", backward)
    return low, high


def six_faces(inner, low, high):
    return jnp.concatenate([inner, low[:, None, :], high[:, None, :]], axis=1)


def invert(matrix_ref, inverse_ref):
    size = matrix_ref.shape[0]
    lane = lax.broadcasted_iota(jnp.int32, (8, size), 1)
    row = lax.broadcasted_iota(jnp.int32, (8, 1), 0)
    tiles = [matrix_ref[8 * t : 8 * t + 8, :] for t in range(size // 8)]
    for k in range(0, size, 2):
        home, at = divmod(k, 8)

        def spread_out(values, place):
            return jnp.broadcast_to(values[:, place : place + 1], (8, size))

        first = jnp.broadcast_to(tiles[home][at : at + 1, :], (8, size))
        second = jnp.broadcast_to(tiles[home][at + 1 : at + 2, :], (8, size))
        across = spread_out(second, k)
        first_part = 1.0 / spread_out(first, k)
        ratio = across * first_part
        second_part = 1.0 / (spread_out(second, k + 1) - ratio * across)
        mixed_part = ratio * second_part
        here, after = lane == k, lane == k + 1
        either = here | after
        first = jnp.where(either, jnp.where(here, 1.0, 0.0), first)
        second = jnp.where(either, jnp.where(after, 1.0, 0.0), second)
        first_scaled = (first_part + ratio * mixed_part) * first - mixed_part * second
        second_scaled = second_part * second - mixed_part * first
        for t, tile in enumerate(tiles):
            first_column, second_column = tile[:, k : k + 1], tile[:, k + 1 : k + 2]
            kept = jnp.where(either, 0.0, tile)
            if t == home:
                pivots = (row == at) | (row == at + 1)
                first_column = jnp.where(pivots, jnp.where(row == at, -1.0, 0.0), first_column)
                second_column = jnp.where(pivots, jnp.where(row == at + 1, -1.0, 0.0), second_column)
                kept = jnp.where(pivots, 0.0, kept)
            tiles[t] = kept - first_column * first_scaled - second_column * second_scaled
    for t, tile in enumerate(tiles):
        inverse_ref[8 * t : 8 * t + 8, :] = tile


def spd_inverse(matrix):
    size = matrix.shape[0]
    return pl.pallas_call(
        invert,
        out_shape=jax.ShapeDtypeStruct((size, size), jnp.float32),
        in_specs=[pl.BlockSpec(memory_space=pltpu.VMEM)],
        out_specs=pl.BlockSpec(memory_space=pltpu.VMEM),
        cost_estimate=pl.CostEstimate(flops=2 * size**3, bytes_accessed=8 * size**2, transcendentals=size),
    )(matrix)


PARTS = 4
VMEM = pl.BlockSpec(memory_space=pltpu.VMEM)


def lane_sum(values):
    return jnp.sum(values, axis=1, keepdims=True)


def row_sum(values):
    return jnp.sum(values, axis=0, keepdims=True)


def advance(count, gathered, image_sum, state, state_out, weighted, rho, weighted_out, rho_out, refs, again):
    spread, mask, by_coarse, by_weighted, by_products, cols, basis, weights = refs
    coarse = weighted.shape[0]
    near = cols.shape[0]
    values = gathered[:, :LANES]
    high = values.astype(jnp.bfloat16)
    rest = values - high.astype(jnp.float32)
    middle = rest.astype(jnp.bfloat16)
    low = (rest - middle.astype(jnp.float32)).astype(jnp.bfloat16)
    lifted = (
        jnp.dot(high, spread[...], preferred_element_type=jnp.float32)
        + jnp.dot(middle, spread[...], preferred_element_type=jnp.float32)
        + jnp.dot(low, spread[...], preferred_element_type=jnp.float32)
    )
    lifted = row_sum(lifted * mask[...])
    coarse_row = lifted[:, :LANES] + lifted[:, LANES : 2 * LANES] + lifted[:, 2 * LANES : 3 * LANES]
    weighted_row = (
        lifted[:, 3 * LANES : 4 * LANES] + lifted[:, 4 * LANES : 5 * LANES] + lifted[:, 5 * LANES :]
    )
    totals = row_sum(values)
    rho_now = rho[:, count : count + 1]
    step = rho_now / totals[:, 36:37]
    from_coarse = lane_sum(by_coarse[...] * coarse_row)
    from_weighted = lane_sum(by_weighted[...] * weighted_row)
    shift = from_coarse[:coarse]
    weighted_shift = from_coarse[coarse : 2 * coarse]
    near_shift = from_coarse[2 * coarse : 2 * coarse + near]
    image = image_sum[...] - row_sum(cols[...] * near_shift)
    direction = state[0:1, :]
    solution = state[1:2, :] + step * direction
    residual = state[2:3, :] - step * image
    if not again:
        state_out[0][...] = solution
        state_out[1][...] = residual
        return
    state_out[1:2, :] = solution
    state_out[2:3, :] = residual
    near_turned = from_coarse[2 * coarse + near : 2 * coarse + 2 * near] + from_weighted[coarse : coarse + near]
    coeff_change = (
        from_coarse[2 * coarse + 2 * near :]
        + from_weighted[coarse + near :]
        + lane_sum(by_products[...] * totals)
    )
    found_weighted = from_weighted[:coarse]
    cross = totals[:, 37:38] - row_sum(shift * weighted[...])
    square = lane_sum(row_sum(gathered[:, LANES:])) - row_sum(shift * (2.0 * found_weighted - weighted_shift))
    rho_next = rho_now - step * (2.0 * cross - step * square)
    weighted_out[...] = weighted[...] - step * (found_weighted - weighted_shift)
    rho_out[...] = jnp.broadcast_to(rho_next, rho_out.shape)
    change = weights[...] * image - row_sum(cols[...] * near_turned) - row_sum(basis[...] * coeff_change)
    deflated = state[3:4, :] - step * change
    state_out[3:4, :] = deflated
    state_out[0:1, :] = deflated + (rho_next / rho_now) * direction


def apply(count, operator, held, arrived, state, tests, images, weights, live, product, sums):
    rows = held.shape[0] // PARTS
    direction = state[0:1, :]
    rounded = jnp.broadcast_to(direction, (16, direction.shape[1])).astype(jnp.bfloat16)
    total = None
    for part in range(PARTS):
        pltpu.make_async_copy(
            operator.at[pl.ds(part * rows, rows)], held.at[pl.ds(part * rows, rows)], arrived.at[part]
        ).wait()
        piece = jnp.dot(
            rounded[:, part * rows : (part + 1) * rows],
            held[part * rows : (part + 1) * rows, :],
            preferred_element_type=jnp.float32,
        )
        total = piece if total is None else total + piece
    found = live[...] * total[0:1, :]
    product[...] = found
    column = jnp.concatenate([lane_sum(tests[...] * found), lane_sum(images[...] * found)], axis=0)
    size = column.shape[0]
    rows_of = lax.broadcasted_iota(jnp.int32, (size, LANES), 0)
    lanes_of = lax.broadcasted_iota(jnp.int32, (size, LANES), 1)
    lane = lax.broadcasted_iota(jnp.int32, (1, LANES), 1)
    row = row_sum(jnp.where(rows_of == lanes_of, column, 0.0))
    row = row + jnp.where(lane == 36, lane_sum(direction * found), 0.0)
    sums[...] = row + jnp.where(lane == 37, lane_sum(weights[...] * state[2:3, :] * found), 0.0)


def fetch(operator, held, arrived):
    rows = held.shape[0] // PARTS
    for part in range(PARTS):
        pltpu.make_async_copy(
            operator.at[pl.ds(part * rows, rows)], held.at[pl.ds(part * rows, rows)], arrived.at[part]
        ).start()


def step_kernel(count, again, *refs):
    if not again:
        gathered, image_sum, state, weighted, rho, *rest = refs
        outs = rest[-2:]
        advance(count, gathered, image_sum, state, outs, weighted, rho, None, None, rest[:-2], False)
        return
    gathered, image_sum, state, weighted, rho = refs[:5]
    shared = refs[5:13]
    operator, tests, images, live = refs[13:17]
    state_out, weighted_out, rho_out, product, sums, held, arrived = refs[17:]
    fetch(operator, held, arrived)
    advance(count, gathered, image_sum, state, state_out, weighted, rho, weighted_out, rho_out, shared, True)
    apply(count, operator, held, arrived, state_out, tests, images, shared[-1], live, product, sums)


def first_kernel(count, state, operator, tests, images, weights, live, product, sums, held, arrived):
    fetch(operator, held, arrived)
    apply(count, operator, held, arrived, state, tests, images, weights, live, product, sums)


def shape_of(*dims):
    return jax.ShapeDtypeStruct(dims, jnp.float32)


def local(dual_ops, neighbors, face_counts, load_terms, precond_terms, rigid_terms, recycled_terms):
    local_op = dual_ops[0, 0]
    neighbor_ids = neighbors[0, 0]
    load = load_terms[0, 0]
    rigid = rigid_terms[0, 0]
    recycled = recycled_terms[0, 0].astype(jnp.float32)
    clusters = lax.axis_size("clu")
    members = lax.axis_size("sub")
    clu_index = lax.axis_index("clu")
    sub_index = lax.axis_index("sub")
    slots = load.shape[-1]
    width = 6 * slots
    count = recycled.shape[0]
    per = count // members
    piece = 4 * per * slots
    coarse = 6 * clusters
    onehot = (neighbor_ids[:, None] == jnp.arange(members, dtype=jnp.int32)[None, :]).astype(
        jnp.float32
    )
    live = (
        jnp.arange(slots, dtype=jnp.int32)[None, :] < face_counts[0, 0][:, None]
    ).astype(jnp.float32)
    flat_live = live.reshape(1, width)

    targets = jnp.arange(coarse, dtype=jnp.int32)[:, None]
    sources = jnp.arange(18 * clusters, dtype=jnp.int32)[None, :]
    spread = (
        targets == 6 * (sources // 18) + (sources % 18) - 6
    ).astype(jnp.float32)
    spread_back = spread.T.reshape(clusters, 18, coarse)

    def nearby(values):
        padded = jnp.pad(values, ((6, 6), (0, 0)))
        return lax.dynamic_slice_in_dim(padded, 6 * clu_index, 18, 0)

    def to_carriers(values):
        faces = values.reshape(members, per, 6, slots)[:, :, :4]
        return faces.transpose(0, 2, 1, 3).reshape(members, piece)

    def from_carriers(received):
        faces = received.reshape(members, 4, per, slots).transpose(0, 2, 1, 3)
        return faces.reshape(count, 4, slots)

    few = jnp.concatenate([load[None], precond_terms[0, 0][None], rigid], axis=0)
    few_count = few.shape[0]
    direct = dot(onehot.T, few[:, :4].transpose(1, 0, 2).reshape(4, few_count * slots))
    ids = jnp.broadcast_to(padded_row(neighbor_ids.astype(jnp.float32))[None], (members, LANES))
    first_blocks = jnp.concatenate([to_carriers(recycled), direct, ids], axis=1)
    few_later, first_blocks = lax.optimization_barrier((few, first_blocks))
    received = trade(first_blocks, "sub")
    few_low, few_high = rims(few_later)
    table = received[:, piece + few_count * slots :][:, :4]
    slots_of = 4 * members
    row_member = (lax.broadcasted_iota(jnp.int32, (slots_of, slots_of), 0) // 4).astype(jnp.float32)
    lane_member = (lax.broadcasted_iota(jnp.int32, (slots_of, slots_of), 1) // 4).astype(jnp.float32)
    route = jnp.where(
        (table.reshape(slots_of, 1) == lane_member) & (table.reshape(1, slots_of) == row_member), 1.0, 0.0
    )

    def carry(arrived):
        return dot(route, arrived.reshape(4 * members, per * slots)).reshape(members, piece)

    few_inner = dot(onehot, received[:, piece : piece + few_count * slots])
    few_inner = few_inner.reshape(4, few_count, slots).transpose(1, 0, 2)
    few_copy = six_faces(few_inner, few_low, few_high)
    demand = (live * (load + few_copy[0])).reshape(1, width)
    weights = (0.5 * live * (few[1] + few_copy[1])).reshape(1, width)
    face_index = jnp.arange(6, dtype=jnp.int32)
    inner_face = (face_index < 4).astype(jnp.float32)[:, None]
    below_face = (face_index == 4).astype(jnp.float32)[:, None]
    above_face = (face_index == 5).astype(jnp.float32)[:, None]
    rigid_copy = few_copy[2:]
    cols = jnp.concatenate(
        [
            live * rigid_copy * below_face,
            live * (rigid + rigid_copy * inner_face),
            live * rigid_copy * above_face,
        ],
        axis=0,
    ).reshape(18, width)
    weighted_cols = weights * cols
    flat_recycled = recycled.reshape(count, width)
    sums = dot_t(
        cols,
        jnp.concatenate(
            [0.5 * cols, 0.5 * weighted_cols, flat_recycled, load.reshape(1, width)], axis=0
        ),
    )
    sums_size = sums.size
    sums_row = padded_row(sums)
    second_blocks = jnp.concatenate(
        [carry(received[:, :piece]), jnp.broadcast_to(sums_row[None], (members, sums_row.shape[0]))],
        axis=1,
    )
    recycled_later, second_blocks = lax.optimization_barrier((recycled, second_blocks))
    received = trade(second_blocks, "sub")
    low, high = rims(recycled_later)
    basis_raw = (
        live * (recycled + six_faces(from_carriers(received[:, :piece]), low, high))
    ).reshape(count, width)
    gathered = everyone(jnp.sum(received[:, piece:], axis=0), "clu")
    gathered = gathered[:, :sums_size].reshape(clusters, 18, 37 + count)
    pairs = jnp.einsum(
        "cgab,cbx->cagx",
        jnp.stack([gathered[:, :, :18], gathered[:, :, 18:36]], axis=1),
        spread_back,
        precision=precise,
    ).reshape(18 * clusters, 2 * coarse)
    assembled = dot(
        spread,
        jnp.concatenate([pairs, gathered[:, :, 36:].reshape(18 * clusters, count + 1)], axis=1),
    )
    coarse_inverse = spd_inverse(assembled[:, :coarse])
    weighted_matrix = assembled[:, coarse : 2 * coarse]
    amounts = nearby(dot(coarse_inverse, assembled[:, 2 * coarse :]))
    projected = jnp.concatenate([basis_raw, demand], axis=0) - dot(amounts.T, cols)
    basis = projected[:count]
    start = projected[count:]

    products = flat_live * jnp.dot(
        basis.astype(jnp.bfloat16), local_op, preferred_element_type=jnp.float32
    )
    both_cols = jnp.concatenate([cols, weighted_cols], axis=0)
    grouped = both_cols.reshape(2, 3, 6, width).transpose(0, 2, 1, 3).reshape(12, 3, width)
    grouped = jnp.pad(grouped, ((0, 0), (0, 1), (0, 0))).reshape(48, width)
    tests = jnp.concatenate([basis, grouped], axis=0)
    sums = dot_t(tests, products)
    start_row = dot_t(0.5 * start, tests)
    basis_parts = count // 4
    shares = jnp.concatenate(
        [
            sums.reshape(basis_parts + 12, 4 * count),
            jnp.pad(start_row[:, :count], ((0, 0), (0, 3 * count))),
            jnp.pad(start_row[:, count:], ((0, 0), (0, 4 * count - 48))),
            jnp.zeros((members - basis_parts - 14, 4 * count), jnp.float32),
        ],
        axis=0,
    )
    blocks = jnp.concatenate([to_carriers(products), shares], axis=1)
    products_later, blocks = lax.optimization_barrier((products, blocks))
    received = trade(blocks, "sub")
    low, high = rims(products_later.reshape(count, 6, slots))
    share = everyone(jnp.sum(received[:, piece:], axis=0), "clu").reshape(clusters, 4, count)
    whole = jnp.pad(jnp.sum(share, axis=0), ((0, clusters - 4), (0, 0)))
    beside = jnp.pad(share[:, :3], ((1, 1), (0, 0), (0, 0)))
    shifted = beside[2:, 0] + beside[1:-1, 1] + beside[:-2, 2]
    is_coarse = (sub_index >= basis_parts) & (sub_index < basis_parts + 12)
    is_listed = sub_index == basis_parts + 13
    share = jnp.where(is_coarse, shifted, jnp.where(is_listed, share[:, 0], whole))
    share_size = clusters * count
    received = trade(
        jnp.concatenate(
            [
                carry(received[:, :piece]),
                jnp.broadcast_to(share.reshape(1, share_size), (members, share_size)),
            ],
            axis=1,
        ),
        "sub",
    )
    images = (
        live
        * (products.reshape(count, 6, slots) + six_faces(from_carriers(received[:, :piece]), low, high))
    ).reshape(count, width)
    parts = received[:, piece:].reshape(members, clusters, count)
    energy_raw = parts[:basis_parts, :4].reshape(count, count)
    image_coarse = parts[basis_parts : basis_parts + 6].transpose(1, 0, 2).reshape(coarse, count)
    image_weighted = parts[basis_parts + 6 : basis_parts + 12].transpose(1, 0, 2).reshape(coarse, count)
    start_sums = parts[basis_parts + 12, 0][:, None]
    listed = parts[basis_parts + 13, :, 24:48].reshape(clusters, 6, 4)[:, :, :3]
    start_weighted = dot(spread, listed.transpose(0, 2, 1).reshape(18 * clusters, 1))
    energy_inverse = spd_inverse(0.5 * (energy_raw + energy_raw.T))
    amount = dot(energy_inverse, start_sums)

    mixed = dot(amount.T, jnp.concatenate([basis, images], axis=1))
    solution = mixed[:, :width]
    shift = dot(coarse_inverse, dot(image_coarse, amount))
    residual = start - mixed[:, width:] + dot(nearby(shift).T, cols)
    weighted_residual = start_weighted - dot(image_weighted, amount) + dot(weighted_matrix, shift)
    amounts = dot(coarse_inverse, weighted_residual)
    search = weights * residual - dot(nearby(amounts).T, cols)
    weighted_images = weights * images
    sums_row = padded_row(
        dot_t(jnp.concatenate([products, 0.5 * residual], axis=0), weights * residual)
    )
    received = everyone(
        jnp.concatenate([sums_row, weights[0, : 4 * slots]]), "sub"
    )
    all_weights = received[:, LANES:].reshape(slots_of, slots)
    to_clusters = jnp.sum(received[:, :LANES], axis=0)
    totals = jnp.sum(everyone(to_clusters, "clu"), axis=0, keepdims=True)
    rho = totals
    (to_clusters, weighted_matrix, coarse_inverse, energy_inverse, image_weighted, image_coarse) = (
        lax.optimization_barrier(
            (to_clusters, weighted_matrix, coarse_inverse, energy_inverse, image_weighted, image_coarse)
        )
    )
    near_rows = lax.broadcasted_iota(jnp.int32, (24, coarse), 0)
    near_lanes = lax.broadcasted_iota(jnp.int32, (24, coarse), 1)
    near_select = ((near_lanes == 6 * clu_index + near_rows - 6) & (near_rows < 18)).astype(jnp.float32)
    weighted_inverse = dot(weighted_matrix, coarse_inverse)
    twice = dot(coarse_inverse, weighted_inverse)
    both_near = dot(near_select, jnp.concatenate([coarse_inverse, twice], axis=1))
    by_shift = dot(energy_inverse, image_weighted.T)
    by_amounts = dot(energy_inverse, image_coarse.T)
    weighted_coeff = -dot(by_amounts, coarse_inverse)
    coarse_coeff = dot(by_amounts, twice) - dot(by_shift, coarse_inverse)
    lane_pad = ((0, 0), (0, LANES - coarse))
    by_coarse = jnp.pad(
        jnp.concatenate(
            [coarse_inverse, weighted_inverse, both_near[:, :coarse], -both_near[:, coarse:], coarse_coeff],
            axis=0,
        ),
        lane_pad,
    )
    by_weighted = jnp.pad(
        jnp.concatenate(
            [jnp.eye(coarse, dtype=jnp.float32), both_near[:, :coarse], weighted_coeff], axis=0
        ),
        lane_pad,
    )
    by_products = jnp.pad(energy_inverse, ((0, 0), (40, LANES - 40 - count)))
    lift_rows = lax.broadcasted_iota(jnp.int32, (LANES, 6 * LANES), 0)
    lift_lanes = lax.broadcasted_iota(jnp.int32, (LANES, 6 * LANES), 1)
    lift = (
        (lift_rows // 6 == lift_lanes // LANES) & (lift_rows % 6 == (lift_lanes % LANES) % 6)
    ).astype(jnp.bfloat16)
    mask_rows = lax.broadcasted_iota(jnp.int32, (clusters, 6 * LANES), 0)
    mask_lanes = lax.broadcasted_iota(jnp.int32, (clusters, 6 * LANES), 1)
    lift_mask = (
        mask_rows + (mask_lanes // LANES) % 3 - 1 == (mask_lanes % LANES) // 6
    ).astype(jnp.float32)
    padded_cols = jnp.pad(cols, ((0, 6), (0, 0)))
    tests = jnp.pad(both_cols, ((0, 4), (0, 0)))

    coeff = dot(energy_inverse, totals[:, :count].T) - dot(by_amounts, amounts)
    deflated_search = search - dot(coeff.T, basis)
    state = jnp.concatenate([deflated_search, solution, residual, deflated_search], axis=0)
    shared = (lift, lift_mask, by_coarse, by_weighted, by_products, padded_cols, basis, weights)
    scratch = [pltpu.VMEM(local_op.shape, jnp.bfloat16), pltpu.SemaphoreType.DMA((PARTS,))]
    params = pltpu.CompilerParams(vmem_limit_bytes=52 * 2**20)
    anywhere = pl.BlockSpec(memory_space=pltpu.HBM)
    cost = pl.CostEstimate(
        flops=2 * width * width, bytes_accessed=2 * width * width + 4 * 300 * width, transcendentals=0
    )
    product, sums = pl.pallas_call(
        functools.partial(first_kernel, count),
        out_shape=(shape_of(1, width), shape_of(1, LANES)),
        in_specs=[VMEM, anywhere, VMEM, VMEM, VMEM, VMEM],
        out_specs=(VMEM, VMEM),
        scratch_shapes=scratch,
        compiler_params=params,
        cost_estimate=cost,
    )(state, local_op, tests, weighted_images, weights, flat_live)
    for iteration in range(ITERS):
        last = iteration + 1 == ITERS
        faces = product.reshape(6, slots)
        low, high = rims(faces[None])
        sent = [product[0, : 4 * slots], sums[0]]
        if not last:
            beside = jnp.concatenate([jnp.zeros((1, 4 * slots), jnp.float32), low, high], axis=1)
            square = weights * product * (product + beside)
            sent.append(jnp.sum(square.reshape(width // LANES, LANES), axis=0))
        received = everyone(jnp.concatenate(sent), "sub")
        all_faces = received[:, : 4 * slots].reshape(slots_of, slots)
        all_partners = dot(route, all_faces)
        inner = lax.dynamic_slice_in_dim(all_partners, 4 * sub_index, 4, 0)
        assembled = (live * (faces + jnp.concatenate([inner, low, high], axis=0))).reshape(1, width)
        sums = jnp.sum(received[:, 4 * slots :], axis=0)
        if not last:
            cross = jnp.sum(all_weights * all_faces * all_partners, axis=0)
            cross = jnp.sum(cross.reshape(slots // LANES, LANES), axis=0)
            sums = sums + jnp.concatenate([jnp.zeros((LANES,), jnp.float32), cross])
        gathered = everyone(sums, "clu")
        ahead = (gathered, assembled, state, weighted_residual, rho)
        if last:
            solution, residual = pl.pallas_call(
                functools.partial(step_kernel, count, False),
                out_shape=(shape_of(1, width), shape_of(1, width)),
                in_specs=[VMEM] * 13,
                out_specs=(VMEM, VMEM),
                compiler_params=params,
            )(*ahead, *shared)
            break
        state, weighted_residual, rho, product, sums = pl.pallas_call(
            functools.partial(step_kernel, count, True),
            out_shape=(
                shape_of(4, width),
                shape_of(coarse, 1),
                shape_of(1, LANES),
                shape_of(1, width),
                shape_of(1, LANES),
            ),
            in_specs=[VMEM] * 13 + [anywhere, VMEM, VMEM, VMEM],
            out_specs=(VMEM,) * 5,
            scratch_shapes=scratch,
            compiler_params=params,
            cost_estimate=cost,
        )(*ahead, *shared, local_op, tests, weighted_images, flat_live)
    return (solution.reshape(1, 1, 6, slots), residual.reshape(1, 1, 6, slots))


def solution(mesh):
    return jax.shard_map(
        local,
        mesh=mesh,
        in_specs=(
            P("clu", "sub", None, None),
            P("clu", "sub", None),
            P("clu", "sub", None),
            P("clu", "sub", None, None),
            P("clu", "sub", None, None),
            P("clu", "sub", None, None, None),
            P("clu", "sub", None, None, None),
        ),
        out_specs=(P("clu", "sub", None, None), P("clu", "sub", None, None)),
        check_vma=False,
    )
```
